256 devices in a mesh: seq: 64 (over y, z, core), fsdp: 4 (over x).
Axes of the slice: x: 4, y: 4, z: 8, core: 2. Of those that a mesh axis runs over, the one named last changes fastest.
Arguments:
- byte_states: bfloat16 [4, 32768, 1024], P('fsdp', 'seq'), may hold values from -6 to 6
- byte_wide: bfloat16 [4, 32768, 4096], P('fsdp', 'seq'), may hold values from -6 to 6
- patch_of: int32 [4, 32768], P('fsdp', 'seq'), may hold values from 0 to 127, as said below
- w_query: bfloat16 [4096, 2048], P('fsdp'), may hold values from -0.09375 to 0.09375
- w_keyval: bfloat16 [4096, 1024], P('fsdp'), may hold values from -0.09375 to 0.09375
- w_out: bfloat16 [1024, 1024], P('fsdp'), may hold values from -0.1875 to 0.1875
- norm_gain: float32 [1024], replicated, may hold values from 0.2 to 3
- out_grad: bfloat16 [4, 32768, 1024], P('fsdp', 'seq'), may hold values from -6 to 6
Outputs:
- grad_weight: float32 [1024, 1024], P('seq')
- grad_gain: float32 [1024], replicated
The draws below stay inside these ranges and needn't reach their ends.
Inputs may be any that keep to these rules, and one draw needn't show every extreme that they name: `patch_of`: within each shard of 512 bytes the ids start at 0 and rise by 0 or 1 from byte to byte; a shard holds from 64 to 128 patches, and in every draw some shard holds exactly 128.
All inputs are finite; a program needn't handle non-finite values.
Results may differ from the reference program's by a relative error of at most 0.02.
Values may be sent and summed in bfloat16 or wider, within the bound.
A program may use at most 128 MiB of HBM per device.

```python
import jax
import jax.numpy as jnp
from jax import lax

C = 1024
D = 4096
HQ = 16
HK = 4
E = 128
BYTE_DEV = 512
PCAP = 128
BATCH = 4
LEN = 32768
PATCHES = 8192
N_SEQ = 64
N_FSDP = 4


def draw_patch_of(key, part):
    key = jax.random.fold_in(key, 7)
    shard_total = N_FSDP * N_SEQ
    key_count, key_pick, key_order = jax.random.split(key, 3)
    counts = jax.random.randint(key_count, (shard_total,), PCAP // 2, PCAP + 1)
    chosen = jax.random.randint(key_pick, (), 0, shard_total)
    counts = jnp.where(jnp.arange(shard_total) == chosen, PCAP, counts)
    scores = jax.random.randint(key_order, (shard_total, BYTE_DEV - 1), 0, 1 << 20) * BYTE_DEV
    scores = scores + jnp.arange(BYTE_DEV - 1, dtype=jnp.int32)[None, :]
    ranks = jnp.argsort(jnp.argsort(scores, axis=1), axis=1)
    cuts = (ranks < (counts - 1)[:, None]).astype(jnp.int32)
    patch_ids = jnp.concatenate([jnp.zeros((shard_total, 1), jnp.int32), jnp.cumsum(cuts, axis=1)], axis=1)
    return patch_ids.astype(jnp.int32).reshape(N_FSDP, N_SEQ * BYTE_DEV)


def draw_norm_gain(key, part):
    key = jax.random.fold_in(key, 11)
    along = jnp.arange(C, dtype=jnp.float32) / float(C - 1)
    rough = jax.random.uniform(key, (C,), jnp.float32, 0.8, 1.2)
    ramp = 0.4 + 1.6 * along
    return (ramp * rough).astype(jnp.float32)


def block_levels(stream_key, shape, shards, least, top_value):
    loudness = 1.0
    for axis_at, blocks in shards:
        heights = jax.random.uniform(jax.random.fold_in(jax.random.fold_in(stream_key, 6), axis_at), (blocks,), jnp.float32, least / len(shards), top_value / len(shards))
        loudness = loudness * jnp.repeat(jnp.exp(heights), shape[axis_at] // blocks).reshape((-1,) + (1,) * (len(shape) - 1 - axis_at))
    return loudness


def scatter_about(key, extent, spread, most, shards=(), held_as=jnp.bfloat16):
    result = jax.random.normal(key, extent, jnp.float32) * spread
    if len(shards) > 0:
        result = block_levels(key, extent, shards, -0.22, 0.18) * result
    return jnp.clip(result, min=-most, max=most).astype(held_as)


def setup_inputs(seed: int = 0) -> dict:
    keys = jax.random.split(jax.random.key(seed), 9)
    return {
        "byte_states": scatter_about(keys[0], (BATCH, LEN, C), 1.0, 6.0, ((0, 4), (1, 64))),
        "byte_wide": scatter_about(keys[1], (BATCH, LEN, D), 1.0, 6.0, ((0, 4), (1, 64))),
        "patch_of": draw_patch_of(jax.random.fold_in(keys[8], 71), 0),
        "w_query": scatter_about(keys[3], (D, HQ * E), D ** -0.5, 0.09375, ((0, 4),)),
        "w_keyval": scatter_about(keys[4], (D, 2 * HK * E), D ** -0.5, 0.09375, ((0, 4),)),
        "w_out": scatter_about(keys[5], (C, C), C ** -0.5, 0.1875, ((0, 4),)),
        "norm_gain": draw_norm_gain(jax.random.fold_in(keys[8], 71), 0),
        "out_grad": scatter_about(keys[7], (BATCH, LEN, C), 1.0, 6.0, ((0, 4), (1, 64))),
    }


epsilon = 1e-05

def reference(byte_states, byte_wide, patch_of, w_query, w_keyval, w_out, norm_gain, out_grad):
    group_size = HQ // HK
    dec_heads = C // E
    attn_scale = float(E) ** (-0.5)
    slot_ids = jnp.arange(PCAP, dtype=jnp.int32)

    def pool_shard(shard_item):
        wide_rows, patch_ids = shard_item
        onehot = (patch_ids[:, None] == slot_ids[None, :]).astype(jnp.bfloat16)
        pool_sums = lax.dot_general(onehot, wide_rows, (((0,), (0,)), ((), ())), preferred_element_type=jnp.float32)
        pool_sizes = lax.optimization_barrier(jnp.sum(onehot.astype(jnp.float32), axis=0))
        return (pool_sums / jnp.maximum(pool_sizes, 1.0)[:, None]).astype(jnp.bfloat16)

    def one_batch(inputs):
        states, wide_rows, patch_ids, cotangent = inputs
        shard_ids = patch_ids.reshape(N_SEQ, BYTE_DEV)
        counts = shard_ids[:, -1] + 1
        pooled = lax.map(pool_shard, (wide_rows.reshape(N_SEQ, BYTE_DEV, D), shard_ids)).reshape(PATCHES, D)
        pooled_f = pooled.astype(jnp.float32)
        normed = (pooled_f * lax.rsqrt(lax.optimization_barrier(jnp.mean(pooled_f * pooled_f, axis=1, keepdims=True)) + epsilon)).astype(jnp.bfloat16)
        queries = jnp.dot(normed, w_query, preferred_element_type=jnp.float32).astype(jnp.bfloat16).reshape(PATCHES, HQ, E)
        keyval = jnp.dot(normed, w_keyval, preferred_element_type=jnp.float32).astype(jnp.bfloat16)
        key_rows = keyval[:, :HK * E].reshape(PATCHES, HK, E)
        value_rows = keyval[:, HK * E:].reshape(PATCHES, HK, E)
        positions = jnp.arange(PATCHES, dtype=jnp.int32)
        live_mask = positions % PCAP < counts[positions // PCAP]
        allowed = live_mask[None, :] & (positions[None, :] <= positions[:, None])

        def one_head(head_index):
            query_head = lax.dynamic_index_in_dim(queries, head_index, axis=1, keepdims=False)
            key_head = lax.dynamic_index_in_dim(key_rows, head_index // group_size, axis=1, keepdims=False)
            value_head = lax.dynamic_index_in_dim(value_rows, head_index // group_size, axis=1, keepdims=False)
            scores = jnp.dot(query_head, key_head.T, preferred_element_type=jnp.float32) * attn_scale
            row_max = lax.optimization_barrier(jnp.max(jnp.where(allowed, scores, -jnp.inf), axis=1))
            expo = jnp.where(allowed, jnp.exp(scores - row_max[:, None]), 0.0)
            denom = lax.optimization_barrier(jnp.sum(expo, axis=1))
            mixed = jnp.dot(expo.astype(jnp.bfloat16), value_head, preferred_element_type=jnp.float32)
            return mixed / denom[:, None]
        attended = lax.map(one_head, jnp.arange(HQ, dtype=jnp.int32))
        attended = jnp.transpose(attended, (1, 0, 2)).reshape(PATCHES, HQ * E)
        ctx = (attended * lax.rsqrt(lax.optimization_barrier(jnp.mean(attended * attended, axis=1, keepdims=True)) + epsilon)).astype(jnp.bfloat16)
        byte_pos = jnp.arange(LEN, dtype=jnp.int32)
        shard_of = byte_pos // BYTE_DEV
        own_index = shard_of * PCAP + patch_ids
        before_shard = jnp.maximum(shard_of - 1, 0)
        prior_index = jnp.where(patch_ids > 0, own_index - 1, before_shard * PCAP + counts[before_shard] - 1)
        has_prior = (patch_ids > 0) | (shard_of > 0)
        prior_index = jnp.where(has_prior, prior_index, 0)
        own_rows = ctx[own_index].astype(jnp.float32)
        prior_rows = ctx[prior_index].astype(jnp.float32)
        query_bytes = states.astype(jnp.float32).reshape(LEN, dec_heads, E)
        own_key = own_rows[:, :C].reshape(LEN, dec_heads, E)
        own_value = own_rows[:, C:].reshape(LEN, dec_heads, E)
        prior_key = prior_rows[:, :C].reshape(LEN, dec_heads, E)
        prior_value = prior_rows[:, C:].reshape(LEN, dec_heads, E)
        own_score = lax.optimization_barrier(jnp.sum(query_bytes * own_key, axis=2)) * attn_scale
        prior_score = jnp.where(has_prior[:, None], lax.optimization_barrier(jnp.sum(query_bytes * prior_key, axis=2)) * attn_scale, -jnp.inf)
        pair_max = jnp.maximum(own_score, prior_score)
        own_exp = jnp.exp(own_score - pair_max)
        prior_exp = jnp.where(has_prior[:, None], jnp.exp(prior_score - pair_max), 0.0)
        attn = (own_exp[..., None] * own_value + prior_exp[..., None] * prior_value) / (own_exp + prior_exp)[..., None]
        outsum = states.astype(jnp.float32) + attn.reshape(LEN, C)
        normal = outsum * lax.rsqrt(lax.optimization_barrier(jnp.mean(outsum * outsum, axis=1, keepdims=True)) + epsilon)
        decoded = (normal * norm_gain[None, :]).astype(jnp.bfloat16)
        weight_part = lax.dot_general(decoded, cotangent, (((0,), (0,)), ((), ())), preferred_element_type=jnp.float32)
        back_rows = lax.dot_general(cotangent, w_out, (((1,), (1,)), ((), ())), preferred_element_type=jnp.float32)
        gain_part = lax.optimization_barrier(jnp.sum(back_rows * normal, axis=0))
        return (weight_part, gain_part)
    weight_parts, gain_parts = lax.map(one_batch, (byte_states, byte_wide, patch_of, out_grad))
    raw_weight = lax.optimization_barrier(jnp.sum(weight_parts, axis=0))
    raw_gain = lax.optimization_barrier(jnp.sum(gain_parts, axis=0))
    grand_total = jnp.sum(raw_weight * raw_weight) + jnp.sum(raw_gain * raw_gain)
    clip_scale = jnp.minimum(1.0, float(C) / jnp.sqrt(grand_total))
    return (raw_weight * clip_scale, raw_gain * clip_scale)
```

```python
import jax
import jax.numpy as jnp
from jax import lax
from jax.experimental import pallas as pl
from jax.experimental.pallas import tpu as pltpu
from jax.sharding import PartitionSpec as P

E = 128
PCAP = 128
NY, NZ, NX = 4, 8, 4
EPS = 1e-05
DEAD_ROW = 1024.0
DEAD_KEY = 4096.0
NEG = -1e30
Q_SCALE = float(E) ** (-0.5) * 1.4426950408889634
MESH = pl.DeviceIdType.MESH
F32 = jnp.float32
BF16 = jnp.bfloat16


def place():
    seq = lax.axis_index("seq")
    return seq // 16, (seq // 2) % 8, seq % 2, lax.axis_index("fsdp")


def dev(y, z, c, x):
    return {"seq": (y * 8 + z) * 2 + c, "fsdp": x}


def greet(peers):
    barrier = pltpu.get_barrier_semaphore()
    for peer in peers:
        pl.semaphore_signal(barrier, inc=1, device_id=peer, device_id_type=MESH)
    pl.semaphore_wait(barrier, len(peers))


def remote(src, dst, send, recv, peer):
    return pltpu.make_async_remote_copy(
        src_ref=src, dst_ref=dst, send_sem=send, recv_sem=recv, device_id=peer, device_id_type=MESH
    )


def dot(a, b, ca=1, cb=0):
    return lax.dot_general(a, b, (((ca,), (cb,)), ((), ())), preferred_element_type=F32)


def iota(shape, axis):
    return lax.broadcasted_iota(jnp.int32, shape, axis)


def project_kernel(ids_ref, wide_ref, wq_ref, wkv_ref, q_ref, kv_ref,
                   wide_v, pooled, nrm, wbuf, acc, lsem, ysend, yrecv, xsend, xrecv, ssend, srecv):
    y, z, c, x = place()
    right, left = dev((y + 1) % 4, z, c, x), dev((y + 3) % 4, z, c, x)
    xright, xleft = dev(y, z, c, (x + 1) % 4), dev(y, z, c, (x + 3) % 4)
    sibling = dev(y, z, 1 - c, x)

    loads = [
        pltpu.make_async_copy(wq_ref.at[:, pl.ds(pl.multiple_of(512 * y, 128), 512)], wbuf.at[0, :, pl.ds(0, 512)], lsem.at[0]),
        pltpu.make_async_copy(wkv_ref.at[:, pl.ds(pl.multiple_of(128 * y, 128), 128)], wbuf.at[0, :, pl.ds(512, 128)], lsem.at[1]),
        pltpu.make_async_copy(wkv_ref.at[:, pl.ds(pl.multiple_of(512 + 128 * y, 128), 128)], wbuf.at[0, :, pl.ds(640, 128)], lsem.at[2]),
    ] + [
        pltpu.make_async_copy(wide_ref.at[:, pl.ds(1024 * k, 1024)], wide_v.at[k], lsem.at[3 + k]) for k in range(4)
    ]
    for load in loads:
        load.start()
    greet([right, left, xright, xleft, sibling])

    def part(slot, owner, half):
        return wbuf.at[slot, pl.ds(pl.multiple_of(512 * owner + 256 * half, 256), 256)]

    for load in loads[:3]:
        load.wait()
    wsends = []
    for direction, peer in ((0, xright), (1, xleft)):
        for half in ((0, 1) if direction == 0 else (1, 0)):
            copy = remote(part(0, c, half), part(1 + direction, c, half),
                          xsend.at[2 * direction + half], xrecv.at[2 * direction + half], peer)
            copy.start()
            wsends.append(copy)

    onehot = (iota((PCAP, 512), 0) == ids_ref[...]).astype(F32)
    sizes = jnp.sum(onehot, axis=1, keepdims=True)
    onehot = onehot.astype(BF16)
    inverse = 1.0 / jnp.maximum(sizes, 1.0)
    squares = jnp.zeros((PCAP, 1), F32)
    for k in range(4):
        loads[3 + k].wait()
        chunk = (dot(onehot, wide_v[k]) * inverse).astype(BF16)
        pooled[k] = chunk
        chunk = chunk.astype(F32)
        squares = squares + jnp.sum(chunk * chunk, axis=1, keepdims=True)
    scale = lax.rsqrt(squares / 4096.0 + EPS)
    for k in range(4):
        chunk = pooled[k].astype(F32) * scale
        if k == 0:
            chunk = jnp.where((iota((PCAP, 1024), 1) == 0) & (sizes < 0.5), DEAD_ROW, chunk)
        nrm[k, 0] = chunk.astype(BF16)

    rows = []
    for first, second in ((0, 3), (1, 2), (2, 1), (3, 0)):
        for direction, peer, k in ((0, right, first), (1, left, second)):
            copy = remote(nrm.at[k, 0], nrm.at[k, 1 + direction],
                          ysend.at[direction, k], yrecv.at[direction, k], peer)
            copy.start()
            rows.append((direction, k, copy))
    arrivals = {(direction, k): copy for direction, k, copy in rows}
    warrivals = {(0, 0): wsends[0], (0, 1): wsends[1], (1, 1): wsends[2], (1, 0): wsends[3]}

    ysends = [copy for _, _, copy in rows]
    lasts, wlasts, ssends = [], [], []

    def give(slot, half):
        i = 2 * (slot - 1) + half
        copy = remote(part(slot, c, half), part(slot, c, half), ssend.at[i], srecv.at[i], sibling)
        copy.start()
        ssends.append(copy)

    def pass_rows(direction, k, peer):
        arrivals[direction, k].wait_recv()
        copy = remote(nrm.at[k, 1 + direction], nrm.at[k, 3], ysend.at[2, k], yrecv.at[2, k], peer)
        copy.start()
        lasts.append(copy)

    def pass_weights(direction, half, peer):
        warrivals[direction, half].wait_recv()
        if peer is not None:
            copy = remote(part(1 + direction, c, half), part(3, c, half), xsend.at[4 + half], xrecv.at[4 + half], peer)
            copy.start()
            wlasts.append(copy)
        give(1 + direction, half)

    pass_weights(0, 0, xright)
    pass_weights(1, 1, xleft)
    pass_rows(0, 0, right)
    pass_rows(1, 3, left)
    pass_rows(0, 1, right)
    pass_rows(1, 2, left)
    pass_weights(0, 1, None)
    pass_weights(1, 0, None)
    for half, copy in enumerate(wlasts):
        copy.wait_recv()
        give(3, half)
    for direction, k in ((0, 2), (1, 1), (0, 3), (1, 0)):
        arrivals[direction, k].wait_recv()
    for slot in (1, 2, 3):
        for half in range(2):
            i = 2 * (slot - 1) + half
            remote(part(slot, 1 - c, half), part(slot, 1 - c, half), ssend.at[i], srecv.at[i], sibling).wait_recv()

    for at, step in enumerate((0, 3, 1, 2)):
        k = (x + step) % 4
        value = dot(nrm[k, 0:3].reshape(384, 1024), wbuf[at])
        if at == 0:
            acc[0:384] = value
        else:
            acc[0:384] += value
    for copy in lasts:
        copy.wait_recv()
    for at, step in enumerate((0, 3, 1, 2)):
        k = (x + step) % 4
        value = dot(nrm[k, 3], wbuf[at])
        if at == 0:
            acc[384:512] = value
        else:
            acc[384:512] += value

    ones = (iota((512, 128), 1) == 0).astype(F32).astype(BF16)
    for slot, step in enumerate((0, 3, 1, 2)):
        at = (y + step) % 4
        here = pl.ds(128 * slot, 128)
        for g in range(4):
            q_ref[at, pl.ds(128 * g, 128), pl.ds(0, 128)] = (acc[here, pl.ds(128 * g, 128)] * Q_SCALE).astype(BF16)
        q_ref[at, :, pl.ds(128, 128)] = ones
        dead = nrm[0, slot][:, 0:128].astype(F32)[:, 0:1] > 512.0
        kv_ref[0, at] = jnp.where(dead, DEAD_KEY, acc[here, pl.ds(512, 128)]).astype(BF16)
        kv_ref[1, at] = acc[here, pl.ds(640, 128)].T.astype(BF16)

    for copy in wsends + wlasts + ysends + lasts + ssends:
        copy.wait_send()


def attend_kernel(ids_ref, q_ref, kv_ref, ctx_ref,
                  blocks, kext, top, total, acc, osend, att, row_out, row_in,
                  zsend, ssend, recv, asend, arecv, rsend, rrecv):
    y, z, c, x = place()
    seq = lax.axis_index("seq")
    sibling = dev(y, z, 1 - c, x)
    dirn = 1 - 2 * c
    za, zb = dev(y, (z + dirn + 8) % 8, c, x), dev(y, (z - dirn + 8) % 8, c, x)
    mates = [dev((y + d) % 4, z, c, x) for d in (1, 2, 3)]
    following = {"seq": (seq + 1) % 64, "fsdp": x}
    before_me = {"seq": (seq + 63) % 64, "fsdp": x}

    blocks[0] = kv_ref[...]
    greet([za, zb, sibling] + mates + [following, before_me])

    first = [
        remote(blocks.at[0], blocks.at[1], zsend.at[1], recv.at[1], za),
        remote(blocks.at[0], blocks.at[2], zsend.at[2], recv.at[2], zb),
        remote(blocks.at[0], blocks.at[8], ssend.at[0], recv.at[8], sibling),
    ]
    for copy in first:
        copy.start()

    def load_keys(slot):
        keys = blocks[slot, 0].reshape(512, 128)
        kext[:, 0:128] = keys
        dead = keys.astype(F32)[:, 0:1] > 2000.0
        kext[:, 128:256] = jnp.broadcast_to(jnp.where(dead, NEG, 0.0), (512, 128)).astype(BF16)

    def update(slot, yq, count, fresh):
        scores = dot(kext[0:128 * count], q_ref[yq], 1, 1)
        if fresh:
            last = scores[128 * (count - 1):]
            allowed = iota((128, 512), 0) <= iota((128, 512), 1) % 128
            last = jnp.where(allowed, last, NEG)
            scores = jnp.concatenate([scores[: 128 * (count - 1)], last], axis=0) if count > 1 else last
        peak = jnp.max(scores, axis=0, keepdims=True)
        if not fresh:
            old = top[yq]
            peak = jnp.maximum(peak, old)
            decay = jnp.exp2(old - peak)
        probs = jnp.exp2(scores - peak)
        sums = jnp.sum(probs, axis=0, keepdims=True)
        values = jnp.concatenate([blocks[slot, 1, i] for i in range(count)], axis=1)
        mixed = dot(values, probs.astype(BF16))
        top[yq] = peak
        if fresh:
            total[yq] = sums
            acc[yq] = mixed
        else:
            total[yq] = total[yq] * decay + sums
            acc[yq] = acc[yq] * decay + mixed

    load_keys(0)
    for yq in range(4):
        update(0, yq, yq + 1, True)

    def item(i, carry):
        s = (i + 1) // 2
        sib = (i + 1) % 2
        slot = s + 8 * sib
        hop = (s + 1) // 2
        odd = s % 2
        remote(blocks.at[slot], blocks.at[slot], zsend.at[1], recv.at[slot], sibling).wait_recv()

        @pl.when((sib == 0) & (s <= 5))
        def _():
            step = dirn * (2 * odd - 1)
            remote(blocks.at[s], blocks.at[s + 2], zsend.at[s + 2], recv.at[s + 2],
                   dev(y, (z + step + 8) % 8, c, x)).start()

        @pl.when(sib == 0)
        def _():
            remote(blocks.at[s], blocks.at[8 + s], ssend.at[s], recv.at[8 + s], sibling).start()

        back = hop * dirn * (1 - 2 * sib) * (2 * odd - 1)
        zsrc = (z - back + 8) % 8
        csrc = (1 - sib) * c + sib * (1 - c)
        earlier = 2 * zsrc + csrc < 2 * z + c
        load_keys(slot)

        @pl.when(earlier)
        def _():
            for yq in range(4):
                update(slot, yq, yq + 1, False)

        @pl.when(jnp.logical_not(earlier))
        def _():
            for yq in range(1, 4):
                update(slot, yq, yq, False)

        return carry

    lax.fori_loop(0, 15, item, 0)

    for yq in range(4):
        out = acc[yq] / total[yq]
        for g in range(4):
            osend[yq, :, pl.ds(128 * g, 128)] = out[:, 128 * g:128 * g + 128].T.astype(BF16)
    sends = []
    for d in (1, 2, 3):
        copy = remote(osend.at[(y + d) % 4], att.at[y], asend.at[d], arecv.at[d], mates[d - 1])
        copy.start()
        sends.append(copy)
    att[y] = osend[y]
    for d, copy in zip((1, 2, 3), sends):
        remote(att.at[(y + 4 - d) % 4], att.at[(y + 4 - d) % 4], asend.at[d], arecv.at[d], mates[d - 1]).wait_recv()

    squares = jnp.zeros((PCAP, 1), F32)
    for h in range(4):
        part = att[h].astype(F32)
        squares = squares + jnp.sum(part * part, axis=1, keepdims=True)
    scale = lax.rsqrt(squares / 2048.0 + EPS)
    final = jnp.max(ids_ref[...].astype(F32), axis=1, keepdims=True).astype(jnp.int32)
    pick = (iota((16, PCAP), 1) == final).astype(F32).astype(BF16)
    for h in range(4):
        ctx = (att[h].astype(F32) * scale).astype(BF16)
        ctx_ref[h, 0:128] = ctx
        row_out[h] = dot(pick, ctx).astype(BF16)
    copy = remote(row_out, row_in, rsend, rrecv, following)
    copy.start()
    copy.wait()
    for h in range(4):
        ctx_ref[h, 128:144] = row_in[h]

    for copy in first + sends:
        copy.wait_send()

    def drain(s, carry):
        remote(blocks.at[s], blocks.at[s], zsend.at[s], recv.at[s], sibling).wait_send()
        return carry

    lax.fori_loop(3, 8, drain, 0)

    def drain_sibling(s, carry):
        remote(blocks.at[s], blocks.at[s], ssend.at[s], recv.at[s], sibling).wait_send()
        return carry

    lax.fori_loop(1, 8, drain_sibling, 0)


def grad_kernel(ids_ref, states_ref, ctx_ref, gain_ref, grad_ref, wout_ref, out_ref, gout_ref,
                sums_t, dec, sib_out, sib_in, y1_out, y2_out, y1_in, y2_in, z_out, z_in, xs, wrow, t1, t2,
                ssend, srecv, ysend, yrecv, zsend, zrecv, xsend, xrecv, wsend, wrecv, asend, arecv, bsend, brecv):
    y, z, c, x = place()
    seq = lax.axis_index("seq")
    me = 2 * z + c
    sibling = dev(y, z, 1 - c, x)
    right, left = dev((y + 1) % 4, z, c, x), dev((y + 3) % 4, z, c, x)
    ymates = [dev((y + d) % 4, z, c, x) for d in (1, 2, 3)]
    xmates = [dev(y, z, c, (x + d) % 4) for d in (1, 2, 3)]
    pmates = [{"seq": 16 * y + (me + d) % 16, "fsdp": x} for d in range(1, 16)]
    greet(ymates + xmates + pmates)

    wcopies = [remote(wout_ref.at[pl.ds(pl.multiple_of(16 * me, 16), 16)], wrow, wsend.at[d], wrecv, xmates[d]) for d in range(3)]

    @pl.when(x == y)
    def _():
        for copy in wcopies:
            copy.start()

    ids = ids_ref[...]
    own_hot = iota((144, 512), 0) == ids
    prior_hot = iota((144, 512), 0) == jnp.where(ids > 0, ids - 1, 128)
    has_prior = (ids > 0) | (seq > 0)
    squares = jnp.zeros((1, 512), F32)
    for h in range(8):
        lanes = pl.ds(128 * (h % 4), 128)
        states = states_ref[:, pl.ds(128 * h, 128)].astype(F32).T
        keys = ctx_ref[h // 4, :, lanes]
        values = ctx_ref[2 + h // 4, :, lanes]
        scores = dot(keys, states.astype(BF16)) * Q_SCALE
        own = jnp.sum(jnp.where(own_hot, scores, 0.0), axis=0, keepdims=True)
        prior = jnp.sum(jnp.where(prior_hot, scores, 0.0), axis=0, keepdims=True)
        prior = jnp.where(has_prior, prior, NEG)
        peak = jnp.maximum(own, prior)
        own = jnp.exp2(own - peak)
        prior = jnp.exp2(prior - peak)
        scale = 1.0 / (own + prior)
        weights = jnp.where(own_hot, own * scale, jnp.where(prior_hot, prior * scale, 0.0))
        attn = dot(values, weights.astype(BF16), 0, 0)
        total = states + attn
        squares = squares + jnp.sum(total * total, axis=0, keepdims=True)
        sums_t[pl.ds(128 * h, 128)] = total
    scale = lax.rsqrt(squares / 1024.0 + EPS)
    for h in range(8):
        gain = jnp.broadcast_to(gain_ref[h:h + 1], (128, 128)).T[:, 0:1]
        rows = ((sums_t[pl.ds(128 * h, 128)] * scale) * gain).astype(BF16)
        for i in range(8):
            at = (h % 2) * 4 + i // 2
            dec[i % 2, h // 2, pl.ds(16 * at, 16)] = rows[16 * i:16 * i + 16]

    order = [(y + 2) % 4, (y + 1) % 4, (y + 3) % 4, y]
    sib_copies = []
    for i, at in enumerate(order):
        sib_out[i] = dot(dec[1 - c, at], grad_ref[...]).astype(BF16)
        copy = remote(sib_out.at[i], sib_in.at[i], ssend.at[i], srecv.at[i], sibling)
        copy.start()
        sib_copies.append(copy)

    def chunk(i):
        mine = dot(dec[c, order[i]], grad_ref[...])
        sib_copies[i].wait_recv()
        return mine + sib_in[i].astype(F32)

    far = chunk(0)
    y1_out[0] = far[:, :512].astype(BF16)
    y1_out[1] = far[:, 512:].astype(BF16)
    ones = [remote(y1_out.at[0], y1_in.at[0], ysend.at[0], yrecv.at[0], right),
            remote(y1_out.at[1], y1_in.at[1], ysend.at[1], yrecv.at[1], left)]
    for copy in ones:
        copy.start()
    to_right = chunk(1)
    to_left = chunk(2)
    ones[0].wait_recv()
    y2_out[0, :, 0:512] = (to_right[:, :512] + y1_in[0].astype(F32)).astype(BF16)
    y2_out[0, :, 512:1024] = to_right[:, 512:].astype(BF16)
    twos = [remote(y2_out.at[0], y2_in.at[0], ysend.at[2], yrecv.at[2], right),
            remote(y2_out.at[1], y2_in.at[1], ysend.at[3], yrecv.at[3], left)]
    twos[0].start()
    ones[1].wait_recv()
    y2_out[1, :, 0:512] = to_left[:, :512].astype(BF16)
    y2_out[1, :, 512:1024] = (to_left[:, 512:] + y1_in[1].astype(F32)).astype(BF16)
    twos[1].start()
    mine = chunk(3)
    for copy in twos:
        copy.wait_recv()
    mine = mine + y2_in[0].astype(F32) + y2_in[1].astype(F32)
    z_out[...] = mine.astype(BF16).reshape(8, 16, 1024)
    z_copies = []
    for d in range(1, 8):
        copy = remote(z_out.at[(z + d) % 8], z_in.at[d], zsend.at[d], zrecv.at[d], dev(y, (z + d) % 8, c, x))
        copy.start()
        z_copies.append(copy)
    rows = z_out[z].astype(F32)
    for d in range(1, 8):
        z_copies[d - 1].wait_recv()
        rows = rows + z_in[d].astype(F32)
    xs[x] = rows
    x_copies = []
    for d in (1, 2, 3):
        copy = remote(xs.at[x], xs.at[x], xsend.at[d], xrecv.at[d], xmates[d - 1])
        copy.start()
        x_copies.append(copy)

    @pl.when(x == y)
    def _():
        wrow[...] = wout_ref[pl.ds(pl.multiple_of(16 * me, 16), 16)]

    @pl.when(x != y)
    def _():
        wcopies[0].wait_recv()

    for d in (1, 2, 3):
        remote(xs.at[(x + 4 - d) % 4], xs.at[(x + 4 - d) % 4], xsend.at[d], xrecv.at[d], xmates[d - 1]).wait_recv()
    rows = (xs[0] + xs[1]) + (xs[2] + xs[3])

    gains = jnp.sum(rows * wrow[...].astype(F32), axis=1, keepdims=True)
    lane = (z % 4) * 32 + c * 16
    spread = jnp.where(iota((16, 128), 1) == iota((16, 128), 0) + lane, gains, 0.0)
    spread = jnp.sum(spread, axis=0, keepdims=True)
    power = jnp.sum(rows * rows, axis=0, keepdims=True)
    parts = power[:, 0:128]
    for i in range(1, 8):
        parts = parts + power[:, 128 * i:128 * i + 128]
    row = iota((8, 128), 0)
    upper = jnp.where(row == 2 * y + z // 4, spread, 0.0) / gain_ref[...]
    t1[me, 0:8] = upper
    t1[me, 8:16] = jnp.where(row == 0, parts, 0.0)
    a_copies = []
    for d in range(1, 16):
        copy = remote(t1.at[me], t1.at[me], asend.at[d], arecv.at[d], pmates[d - 1])
        copy.start()
        a_copies.append(copy)
    for d in range(1, 16):
        there = (me + 16 - d) % 16
        remote(t1.at[there], t1.at[there], asend.at[d], arecv.at[d], pmates[d - 1]).wait_recv()
    tile = t1[0]
    for i in range(1, 16):
        tile = tile + t1[i]
    t2[y] = tile
    b_copies = []
    for d in (1, 2, 3):
        copy = remote(t2.at[y], t2.at[y], bsend.at[d], brecv.at[d], ymates[d - 1])
        copy.start()
        b_copies.append(copy)
    for d in (1, 2, 3):
        there = (y + 4 - d) % 4
        remote(t2.at[there], t2.at[there], bsend.at[d], brecv.at[d], ymates[d - 1]).wait_recv()
    tile = (t2[0] + t2[1]) + (t2[2] + t2[3])
    gsum = tile[0:8]
    grand = jnp.sum(tile[8:16] + gsum * gsum, axis=0, keepdims=True)
    grand = jnp.sum(grand, axis=1, keepdims=True)
    clip = jnp.minimum(1.0, 1024.0 / jnp.sqrt(grand))
    out_ref[...] = rows * clip
    gout_ref[...] = gsum * clip

    for copy in sib_copies + ones + twos + z_copies + x_copies + a_copies + b_copies:
        copy.wait_send()

    @pl.when(x == y)
    def _():
        for copy in wcopies:
            copy.wait_send()


VMEM = pl.BlockSpec(memory_space=pltpu.VMEM)
ANY = pl.BlockSpec(memory_space=pl.ANY)
DMA = pltpu.SemaphoreType.DMA


def params(number):
    return pltpu.CompilerParams(collective_id=number, has_side_effects=True, vmem_limit_bytes=56 * 1024 * 1024)


def project(ids, wide, wq, wkv):
    return pl.pallas_call(
        project_kernel,
        out_shape=[jax.ShapeDtypeStruct((4, 512, 256), BF16), jax.ShapeDtypeStruct((2, 4, 128, 128), BF16)],
        in_specs=[VMEM, ANY, ANY, ANY],
        out_specs=[VMEM, VMEM],
        scratch_shapes=[
            pltpu.VMEM((4, 512, 1024), BF16),
            pltpu.VMEM((4, 128, 1024), BF16),
            pltpu.VMEM((4, 4, 128, 1024), BF16),
            pltpu.VMEM((4, 1024, 768), BF16),
            pltpu.VMEM((512, 768), F32),
            DMA((7,)), DMA((3, 4)), DMA((3, 4)), DMA((6,)), DMA((6,)), DMA((6,)), DMA((6,)),
        ],
        compiler_params=params(0),
        name="project",
    )(ids, wide, wq, wkv)


def attend(ids, q, kv):
    return pl.pallas_call(
        attend_kernel,
        out_shape=jax.ShapeDtypeStruct((4, 144, 512), BF16),
        in_specs=[VMEM] * 3,
        out_specs=VMEM,
        scratch_shapes=[
            pltpu.VMEM((16, 2, 4, 128, 128), BF16),
            pltpu.VMEM((512, 256), BF16),
            pltpu.VMEM((4, 1, 512), F32),
            pltpu.VMEM((4, 1, 512), F32),
            pltpu.VMEM((4, 128, 512), F32),
            pltpu.VMEM((4, 128, 512), BF16),
            pltpu.VMEM((4, 128, 512), BF16),
            pltpu.VMEM((4, 16, 512), BF16),
            pltpu.VMEM((4, 16, 512), BF16),
            DMA((8,)), DMA((8,)), DMA((16,)), DMA((4,)), DMA((4,)), DMA, DMA,
        ],
        compiler_params=params(1),
        name="attend",
    )(ids, q, kv)


def gradient(ids, states, ctx, gain, grad, wout):
    return pl.pallas_call(
        grad_kernel,
        out_shape=[jax.ShapeDtypeStruct((16, 1024), F32), jax.ShapeDtypeStruct((8, 128), F32)],
        in_specs=[VMEM] * 6,
        out_specs=[VMEM, VMEM],
        scratch_shapes=[
            pltpu.VMEM((1024, 512), F32),
            pltpu.VMEM((2, 4, 128, 512), BF16),
            pltpu.VMEM((4, 128, 1024), BF16),
            pltpu.VMEM((4, 128, 1024), BF16),
            pltpu.VMEM((2, 128, 512), BF16),
            pltpu.VMEM((2, 128, 1024), BF16),
            pltpu.VMEM((2, 128, 512), BF16),
            pltpu.VMEM((2, 128, 1024), BF16),
            pltpu.VMEM((8, 16, 1024), BF16),
            pltpu.VMEM((8, 16, 1024), BF16),
            pltpu.VMEM((4, 16, 1024), F32),
            pltpu.VMEM((16, 1024), BF16),
            pltpu.VMEM((16, 16, 128), F32),
            pltpu.VMEM((4, 16, 128), F32),
            DMA((4,)), DMA((4,)), DMA((4,)), DMA((4,)), DMA((8,)), DMA((8,)), DMA((4,)), DMA((4,)),
            DMA((3,)), DMA, DMA((16,)), DMA((16,)), DMA((4,)), DMA((4,)),
        ],
        compiler_params=params(2),
        name="gradient",
    )(ids, states, ctx, gain, grad, wout)


def on_device(byte_states, byte_wide, patch_of, w_query, w_keyval, w_out, norm_gain, out_grad):
    q, kv = project(patch_of, byte_wide[0], w_query, w_keyval)
    ctx = attend(patch_of, q, kv)
    rows, gains = gradient(patch_of, byte_states[0], ctx, norm_gain.reshape(8, 128), out_grad[0], w_out)
    return rows, gains.reshape(1024)


def solution(mesh):
    return jax.shard_map(
        on_device,
        mesh=mesh,
        in_specs=(
            P("fsdp", "seq", None),
            P("fsdp", "seq", None),
            P("fsdp", "seq"),
            P("fsdp", None),
            P("fsdp", None),
            P("fsdp", None),
            P(),
            P("fsdp", "seq", None),
        ),
        out_specs=(P("seq", None), P()),
        check_vma=False,
    )
```

```python
import jax
import jax.numpy as jnp
from jax import lax
from jax.experimental import pallas as pl
from jax.experimental.pallas import tpu as pltpu
from jax.sharding import PartitionSpec as P

E = 128
PCAP = 128
NY, NZ, NX = 4, 8, 4
EPS = 1e-05
DEAD_ROW = 1024.0
DEAD_KEY = 4096.0
NEG = -1e30
Q_SCALE = float(E) ** (-0.5) * 1.4426950408889634
MESH = pl.DeviceIdType.MESH
F32 = jnp.float32
BF16 = jnp.bfloat16


def place():
    seq = lax.axis_index("seq")
    return seq // 16, (seq // 2) % 8, seq % 2, lax.axis_index("fsdp")


def dev(y, z, c, x):
    return {"seq": (y * 8 + z) * 2 + c, "fsdp": x}


def remote(src, dst, send, recv, peer):
    return pltpu.make_async_remote_copy(
        src_ref=src, dst_ref=dst, send_sem=send, recv_sem=recv, device_id=peer, device_id_type=MESH
    )


def dot(a, b, ca=1, cb=0):
    return lax.dot_general(a, b, (((ca,), (cb,)), ((), ())), preferred_element_type=F32)


def iota(shape, axis):
    return lax.broadcasted_iota(jnp.int32, shape, axis)


STEPS = (0, 3, 1, 2)


def window_kernel(ids_ref, gain_ref, wide_ref, wq_ref, wkv_ref, states_hbm, grad_hbm, wout_ref, out_ref, gout_ref,
                  wide_v, pooled, nrm, wbuf, accp, q_ref, blocks, kext, top, total, acc, osend, att, ctx_ref, row_out, row_in,
                  states_ref, grad_ref, sums_t, dec, sib_out, sib_in, xy_out, xy_in, z_out, z_in, xs, wrow, t0, t1, t2,
                  lsem, ysend, yrecv, xsend, xrecv, ssend, srecv, zrsend, zrsib, zrrecv, asend, arecv, rsend, rrecv,
                  sbsend, sbrecv, xysend, xyrecv, zsend, zrecv, gsend, grecv, wsend, wrecv, fsend, frecv):
    y, z, c, x = place()
    seq = lax.axis_index("seq")
    me = 2 * z + c
    right, left = dev((y + 1) % 4, z, c, x), dev((y + 3) % 4, z, c, x)
    xright, xleft = dev(y, z, c, (x + 1) % 4), dev(y, z, c, (x + 3) % 4)
    sibling = dev(y, z, 1 - c, x)
    ymates = [dev((y + d) % 4, z, c, x) for d in (1, 2, 3)]
    xmates = [dev(y, z, c, (x + d) % 4) for d in (1, 2, 3)]
    zmates = [dev(y, (z + d) % 8, c, x) for d in range(1, 8)]
    diagonals = [dev((y + dy) % 4, z, c, (x + dx) % 4) for dy in (1, 2, 3) for dx in (1, 2, 3)]
    following = {"seq": (seq + 1) % 64, "fsdp": x}
    before_me = {"seq": (seq + 63) % 64, "fsdp": x}
    dirn = 1 - 2 * c
    za, zb = dev(y, (z + dirn + 8) % 8, c, x), dev(y, (z - dirn + 8) % 8, c, x)
    peers = ymates + xmates + zmates + diagonals + [sibling, following, before_me]

    loads = [
        pltpu.make_async_copy(wide_ref.at[:, pl.ds(1024 * k, 1024)], wide_v.at[k], lsem.at[3 + k]) for k in range(4)
    ] + [
        pltpu.make_async_copy(wq_ref.at[:, pl.ds(pl.multiple_of(512 * y, 128), 512)], wbuf.at[0, :, pl.ds(0, 512)], lsem.at[0]),
        pltpu.make_async_copy(wkv_ref.at[:, pl.ds(pl.multiple_of(128 * y, 128), 128)], wbuf.at[0, :, pl.ds(512, 128)], lsem.at[1]),
        pltpu.make_async_copy(wkv_ref.at[:, pl.ds(pl.multiple_of(512 + 128 * y, 128), 128)], wbuf.at[0, :, pl.ds(640, 128)], lsem.at[2]),
        pltpu.make_async_copy(states_hbm, states_ref, lsem.at[7]),
        pltpu.make_async_copy(grad_hbm, grad_ref, lsem.at[8]),
    ]
    for load in loads:
        load.start()
    barrier = pltpu.get_barrier_semaphore()
    for peer in peers:
        pl.semaphore_signal(barrier, inc=1, device_id=peer, device_id_type=MESH)

    onehot = (iota((PCAP, 512), 0) == ids_ref[...]).astype(F32)
    sizes = jnp.sum(onehot, axis=1, keepdims=True)
    onehot = onehot.astype(BF16)
    inverse = 1.0 / jnp.maximum(sizes, 1.0)
    squares = jnp.zeros((PCAP, 1), F32)
    for k in range(4):
        loads[k].wait()
        chunk = (dot(onehot, wide_v[k]) * inverse).astype(BF16)
        pooled[k] = chunk
        chunk = chunk.astype(F32)
        squares = squares + jnp.sum(chunk * chunk, axis=1, keepdims=True)
    for load in loads[4:7]:
        load.wait()
    pl.semaphore_wait(barrier, len(peers))

    def part(slot, owner, half):
        return wbuf.at[slot, pl.ds(pl.multiple_of(512 * owner + 256 * half, 256), 256)]

    wsends = []
    for direction, peer in ((0, xright), (1, xleft)):
        for half in ((0, 1) if direction == 0 else (1, 0)):
            copy = remote(part(0, c, half), part(1 + direction, c, half),
                          xsend.at[2 * direction + half], xrecv.at[2 * direction + half], peer)
            copy.start()
            wsends.append(copy)

    scale = lax.rsqrt(squares / 4096.0 + EPS)
    rows = []
    for pair in ((0, 3), (1, 2)):
        for k in pair:
            chunk = pooled[k].astype(F32) * scale
            if k == 0:
                chunk = jnp.where((iota((PCAP, 1024), 1) == 0) & (sizes < 0.5), DEAD_ROW, chunk)
            nrm[k, 0] = chunk.astype(BF16)
            direction = 0 if k < 2 else 1
            copy = remote(nrm.at[k, 0], nrm.at[k, 1 + direction],
                          ysend.at[direction, k], yrecv.at[direction, k], (right, left)[direction])
            copy.start()
            rows.append((direction, k, copy))
    for direction, k in ((0, 2), (1, 1), (0, 3), (1, 0)):
        copy = remote(nrm.at[k, 0], nrm.at[k, 1 + direction],
                      ysend.at[direction, k], yrecv.at[direction, k], (right, left)[direction])
        copy.start()
        rows.append((direction, k, copy))
    wcopies = [remote(wout_ref.at[pl.ds(pl.multiple_of(16 * me, 16), 16)], wrow, wsend.at[d], wrecv, xmates[d]) for d in range(3)]
    wown = pltpu.make_async_copy(wout_ref.at[pl.ds(pl.multiple_of(16 * me, 16), 16)], wrow, lsem.at[9])

    @pl.when(x == y)
    def _():
        for copy in wcopies:
            copy.start()
        wown.start()

    arrivals = {(direction, k): copy for direction, k, copy in rows}
    warrivals = {(0, 0): wsends[0], (0, 1): wsends[1], (1, 1): wsends[2], (1, 0): wsends[3]}
    ysends = [copy for _, _, copy in rows]
    lasts, wlasts, ssends = [], [], []

    def give(slot, half):
        i = 2 * (slot - 1) + half
        copy = remote(part(slot, c, half), part(slot, c, half), ssend.at[i], srecv.at[i], sibling)
        copy.start()
        ssends.append(copy)

    def pass_rows(direction, k, peer):
        arrivals[direction, k].wait_recv()
        copy = remote(nrm.at[k, 1 + direction], nrm.at[k, 3], ysend.at[2, k], yrecv.at[2, k], peer)
        copy.start()
        lasts.append(copy)

    def pass_weights(direction, half, peer):
        warrivals[direction, half].wait_recv()
        if peer is not None:
            copy = remote(part(1 + direction, c, half), part(3, c, half), xsend.at[4 + half], xrecv.at[4 + half], peer)
            copy.start()
            wlasts.append(copy)
        give(1 + direction, half)

    pass_weights(0, 0, xright)
    pass_weights(1, 1, xleft)
    pass_rows(0, 0, right)
    pass_rows(1, 3, left)
    pass_rows(0, 1, right)
    pass_rows(1, 2, left)
    pass_weights(0, 1, None)
    pass_weights(1, 0, None)
    for half, copy in enumerate(wlasts):
        copy.wait_recv()
        give(3, half)
    for direction, k in ((0, 2), (1, 1), (0, 3), (1, 0)):
        arrivals[direction, k].wait_recv()
    for slot in (1, 2, 3):
        for half in range(2):
            i = 2 * (slot - 1) + half
            remote(part(slot, 1 - c, half), part(slot, 1 - c, half), ssend.at[i], srecv.at[i], sibling).wait_recv()

    ones = (iota((512, 128), 1) == 0).astype(F32).astype(BF16)
    first = []

    def publish(p):
        at = (y + STEPS[p]) % 4
        here = pl.ds(128 * p, 128)
        dead = nrm[0, p][:, 0:128].astype(F32)[:, 0:1] > 512.0
        blocks[0, at, 0] = jnp.where(dead, DEAD_KEY, accp[here, pl.ds(512, 128)]).astype(BF16)
        blocks[0, at, 1] = accp[here, pl.ds(640, 128)].T.astype(BF16)
        for copy in (
            remote(blocks.at[0, at], blocks.at[1, at], zrsend.at[1, p], zrrecv.at[1, p], za),
            remote(blocks.at[0, at], blocks.at[2, at], zrsend.at[2, p], zrrecv.at[2, p], zb),
            remote(blocks.at[0, at], blocks.at[8, at], zrsib.at[0, p], zrrecv.at[8, p], sibling),
        ):
            copy.start()
            first.append(copy)

    def queries(p):
        at = (y + STEPS[p]) % 4
        here = pl.ds(128 * p, 128)
        for g in range(4):
            q_ref[at, pl.ds(128 * g, 128), pl.ds(0, 128)] = (accp[here, pl.ds(128 * g, 128)] * Q_SCALE).astype(BF16)
        q_ref[at, :, pl.ds(128, 128)] = ones

    for at, step in enumerate(STEPS):
        k = (x + step) % 4
        value = dot(nrm[k, 0:3].reshape(384, 1024), wbuf[at])
        if at == 0:
            accp[0:384] = value
        else:
            accp[0:384] += value
    for p in range(3):
        publish(p)
    for p in range(3):
        queries(p)
    for copy in lasts:
        copy.wait_recv()
    for at, step in enumerate(STEPS):
        k = (x + step) % 4
        value = dot(nrm[k, 3], wbuf[at])
        if at == 0:
            accp[384:512] = value
        else:
            accp[384:512] += value
    publish(3)
    queries(3)

    def load_keys(slot):
        for i in range(4):
            keys = blocks[slot, i, 0]
            here = pl.ds(128 * i, 128)
            kext[here, 0:128] = keys
            dead = keys.astype(F32)[:, 0:1] > 2000.0
            kext[here, 128:256] = jnp.broadcast_to(jnp.where(dead, NEG, 0.0), (128, 128)).astype(BF16)

    def group(slot, work, fresh):
        def score(item):
            yq, count = item
            return dot(kext[0:128 * count], q_ref[yq], 1, 1)

        def soften(item, scores):
            yq, count = item
            if fresh:
                last = scores[128 * (count - 1):]
                allowed = iota((128, 512), 0) <= iota((128, 512), 1) % 128
                last = jnp.where(allowed, last, NEG)
                scores = jnp.concatenate([scores[: 128 * (count - 1)], last], axis=0) if count > 1 else last
            peak = jnp.max(scores, axis=0, keepdims=True)
            decay = None
            if not fresh:
                old = top[yq]
                peak = jnp.maximum(peak, old)
                decay = jnp.exp2(old - peak)
            probs = jnp.exp2(scores - peak)
            sums = jnp.sum(probs, axis=0, keepdims=True)
            top[yq] = peak
            total[yq] = sums if fresh else total[yq] * decay + sums
            return probs.astype(BF16), decay

        def mix(item, probs, decay):
            yq, count = item
            values = jnp.concatenate([blocks[slot, i, 1] for i in range(count)], axis=1)
            mixed = dot(values, probs)
            acc[yq] = mixed if fresh else acc[yq] * decay + mixed

        ahead, held = score(work[0]), None
        for i, item in enumerate(work):
            scores = ahead
            if i + 1 < len(work):
                ahead = score(work[i + 1])
            softened = soften(item, scores)
            if held is not None:
                mix(*held)
            held = (item, *softened)
        mix(*held)

    load_keys(0)
    group(0, [(yq, yq + 1) for yq in range(4)], True)

    def ring(i, carry):
        s = (i + 1) // 2
        sib = (i + 1) % 2
        slot = s + 8 * sib
        hop = (s + 1) // 2
        odd = s % 2
        step = dirn * (2 * odd - 1)
        onward = dev(y, (z + step + 8) % 8, c, x)
        for p in range(4):
            at = (y + STEPS[p]) % 4
            remote(blocks.at[slot, at], blocks.at[slot, at], zrsend.at[1, p], zrrecv.at[slot, p], sibling).wait_recv()

            @pl.when((sib == 0) & (s <= 5))
            def _():
                remote(blocks.at[s, at], blocks.at[s + 2, at], zrsend.at[s + 2, p], zrrecv.at[s + 2, p], onward).start()

            @pl.when(sib == 0)
            def _():
                remote(blocks.at[s, at], blocks.at[8 + s, at], zrsib.at[s, p], zrrecv.at[8 + s, p], sibling).start()

        back = hop * dirn * (1 - 2 * sib) * (2 * odd - 1)
        zsrc = (z - back + 8) % 8
        csrc = (1 - sib) * c + sib * (1 - c)
        earlier = 2 * zsrc + csrc < 2 * z + c
        load_keys(slot)

        @pl.when(earlier)
        def _():
            group(slot, [(yq, yq + 1) for yq in range(4)], False)

        @pl.when(jnp.logical_not(earlier))
        def _():
            group(slot, [(yq, yq) for yq in range(1, 4)], False)

        return carry

    lax.fori_loop(0, 15, ring, 0)

    for yq in range(4):
        out = acc[yq] / total[yq]
        for g in range(4):
            osend[yq, :, pl.ds(128 * g, 128)] = out[:, 128 * g:128 * g + 128].T.astype(BF16)
    backs = []
    for d in (2, 1, 3):
        copy = remote(osend.at[(y + d) % 4], att.at[y], asend.at[d], arecv.at[d], ymates[d - 1])
        copy.start()
        backs.append(copy)
    att[y] = osend[y]
    for d in (1, 3, 2):
        there = (y + 4 - d) % 4
        remote(att.at[there], att.at[there], asend.at[d], arecv.at[d], ymates[d - 1]).wait_recv()

    squares = jnp.zeros((PCAP, 1), F32)
    for h in range(4):
        piece = att[h].astype(F32)
        squares = squares + jnp.sum(piece * piece, axis=1, keepdims=True)
    scale = lax.rsqrt(squares / 2048.0 + EPS)
    ids = ids_ref[...]
    final = jnp.max(ids.astype(F32), axis=1, keepdims=True).astype(jnp.int32)
    pick = (iota((16, PCAP), 1) == final).astype(F32).astype(BF16)
    for h in range(4):
        ctx = (att[h].astype(F32) * scale).astype(BF16)
        ctx_ref[h, 0:128] = ctx
        row_out[h] = dot(pick, ctx).astype(BF16)
    row_copy = remote(row_out, row_in, rsend, rrecv, following)
    row_copy.start()
    for load in loads[7:]:
        load.wait()

    own_hot = iota((144, 512), 0) == ids
    prior_hot = iota((144, 512), 0) == jnp.where(ids > 0, ids - 1, 128)
    has_prior = (ids > 0) | (seq > 0)
    row_copy.wait_recv()
    for h in range(4):
        ctx_ref[h, 128:144] = row_in[h]
    squares = jnp.zeros((1, 512), F32)
    for h in range(8):
        lanes = pl.ds(128 * (h % 4), 128)
        states = states_ref[:, pl.ds(128 * h, 128)].astype(F32).T
        keys = ctx_ref[h // 4, :, lanes]
        values = ctx_ref[2 + h // 4, :, lanes]
        scores = dot(keys, states.astype(BF16)) * Q_SCALE
        own = jnp.sum(jnp.where(own_hot, scores, 0.0), axis=0, keepdims=True)
        prior = jnp.sum(jnp.where(prior_hot, scores, 0.0), axis=0, keepdims=True)
        prior = jnp.where(has_prior, prior, NEG)
        peak = jnp.maximum(own, prior)
        own = jnp.exp2(own - peak)
        prior = jnp.exp2(prior - peak)
        scale = 1.0 / (own + prior)
        weights = jnp.where(own_hot, own * scale, jnp.where(prior_hot, prior * scale, 0.0))
        attn = dot(values, weights.astype(BF16), 0, 0)
        summed = states + attn
        squares = squares + jnp.sum(summed * summed, axis=0, keepdims=True)
        sums_t[pl.ds(128 * h, 128)] = summed
    scale = lax.rsqrt(squares / 1024.0 + EPS)
    for h in range(8):
        gain = jnp.broadcast_to(gain_ref[h:h + 1], (128, 128)).T[:, 0:1]
        decoded = ((sums_t[pl.ds(128 * h, 128)] * scale) * gain).astype(BF16)
        for i in range(8):
            at = (h % 2) * 4 + i // 2
            dec[i % 2, h // 2, pl.ds(16 * at, 16)] = decoded[16 * i:16 * i + 16]

    sib_copies = []
    for i, d in enumerate((2, 1, 3, 0)):
        sib_out[i] = dot(dec[1 - c, (y + d) % 4], grad_ref[...]).astype(BF16)
        copy = remote(sib_out.at[i], sib_in.at[i], sbsend.at[i], sbrecv.at[i], sibling)
        copy.start()
        sib_copies.append(copy)
    xy_copies = []
    for i, d in enumerate((2, 1, 3, 0)):
        mine = dot(dec[c, (y + d) % 4], grad_ref[...])
        sib_copies[i].wait_recv()
        mine = mine + sib_in[i].astype(F32)
        for j in range(4):
            xy_out[d, j] = mine[:, 256 * j:256 * j + 256].astype(BF16)
        for e in (2, 1, 3, 0):
            if d == 0 and e == 0:
                continue
            peer = dev((y + d) % 4, z, c, (x + e) % 4)
            copy = remote(xy_out.at[d, (x + e) % 4], xy_in.at[4 * d + e], xysend.at[4 * d + e], xyrecv.at[4 * d + e], peer)
            copy.start()
            xy_copies.append((4 * d + e, copy))
    mine = xy_out[0, x].astype(F32)
    for i, copy in sorted(xy_copies, key=lambda pair: pair[0]):
        copy.wait_recv()
        mine = mine + xy_in[i].astype(F32)
    z_out[...] = mine.astype(BF16).reshape(8, 16, 256)
    z_copies = []
    for d in (4, 3, 5, 2, 6, 1, 7):
        copy = remote(z_out.at[(z + d) % 8], z_in.at[d], zsend.at[d], zrecv.at[d], zmates[d - 1])
        copy.start()
        z_copies.append((d, copy))
    piece = z_out[z].astype(F32)
    for d, copy in sorted(z_copies, key=lambda pair: pair[0]):
        copy.wait_recv()
        piece = piece + z_in[d].astype(F32)
    xs[x] = piece
    x_copies = []
    for d in (2, 1, 3):
        copy = remote(xs.at[x], xs.at[x], gsend.at[d], grecv.at[d], xmates[d - 1])
        copy.start()
        x_copies.append(copy)

    @pl.when(x == y)
    def _():
        wown.wait()

    @pl.when(x != y)
    def _():
        wcopies[0].wait_recv()

    for d in (1, 3, 2):
        there = (x + 4 - d) % 4
        remote(xs.at[there], xs.at[there], gsend.at[d], grecv.at[d], xmates[d - 1]).wait_recv()

    gains = jnp.zeros((16, 1), F32)
    parts = jnp.zeros((1, 128), F32)
    for j in range(4):
        piece = xs[j]
        gains = gains + jnp.sum(piece * wrow[:, pl.ds(256 * j, 256)].astype(F32), axis=1, keepdims=True)
        power = jnp.sum(piece * piece, axis=0, keepdims=True)
        parts = parts + (power[:, 0:128] + power[:, 128:256])
    lane = (z % 4) * 32 + c * 16
    spread = jnp.where(iota((16, 128), 1) == iota((16, 128), 0) + lane, gains, 0.0)
    spread = jnp.sum(spread, axis=0, keepdims=True)
    row = iota((8, 128), 0)
    t0[0, 0:8] = jnp.where(row == 2 * y + z // 4, spread, 0.0) / gain_ref[...]
    t0[0, 8:16] = jnp.where(row == 0, parts, 0.0)
    f_copies = [remote(t0.at[0], t0.at[1], fsend.at[0], frecv.at[0], sibling)]
    f_copies[0].start()
    f_copies[0].wait_recv()
    t1[z] = t0[0] + t0[1]
    for d in (4, 3, 5, 2, 6, 1, 7):
        copy = remote(t1.at[z], t1.at[z], fsend.at[d], frecv.at[d], zmates[d - 1])
        copy.start()
        f_copies.append(copy)
    for d in range(1, 8):
        there = (z + 8 - d) % 8
        remote(t1.at[there], t1.at[there], fsend.at[d], frecv.at[d], zmates[d - 1]).wait_recv()
    tile = t1[0]
    for i in range(1, 8):
        tile = tile + t1[i]
    t2[y] = tile
    for d in (2, 1, 3):
        copy = remote(t2.at[y], t2.at[y], fsend.at[7 + d], frecv.at[7 + d], ymates[d - 1])
        copy.start()
        f_copies.append(copy)
    for d in (1, 2, 3):
        there = (y + 4 - d) % 4
        remote(t2.at[there], t2.at[there], fsend.at[7 + d], frecv.at[7 + d], ymates[d - 1]).wait_recv()
    tile = (t2[0] + t2[1]) + (t2[2] + t2[3])
    gsum = tile[0:8]
    grand = jnp.sum(tile[8:16] + gsum * gsum, axis=0, keepdims=True)
    grand = jnp.sum(grand, axis=1, keepdims=True)
    clip = jnp.minimum(1.0, 1024.0 / jnp.sqrt(grand))
    for j in range(4):
        out_ref[:, pl.ds(256 * j, 256)] = xs[j] * clip
    gout_ref[...] = gsum * clip

    for copy in (wsends + wlasts + ysends + lasts + ssends + first + backs + [row_copy] + sib_copies + x_copies + f_copies
                 + [copy for _, copy in xy_copies] + [copy for _, copy in z_copies]):
        copy.wait_send()

    def drain(s, carry):
        for p in range(4):
            @pl.when(s >= 3)
            def _():
                remote(blocks.at[s, p], blocks.at[s, p], zrsend.at[s, p], zrrecv.at[s, p], sibling).wait_send()
            remote(blocks.at[s, p], blocks.at[s, p], zrsib.at[s, p], zrrecv.at[s, p], sibling).wait_send()
        return carry

    lax.fori_loop(1, 8, drain, 0)

    @pl.when(x == y)
    def _():
        for copy in wcopies:
            copy.wait_send()


VMEM = pl.BlockSpec(memory_space=pltpu.VMEM)
ANY = pl.BlockSpec(memory_space=pl.ANY)
DMA = pltpu.SemaphoreType.DMA


def window(ids, gain, wide, wq, wkv, states, grad, wout):
    return pl.pallas_call(
        window_kernel,
        out_shape=[jax.ShapeDtypeStruct((16, 1024), F32), jax.ShapeDtypeStruct((8, 128), F32)],
        in_specs=[VMEM] * 2 + [ANY] * 6,
        out_specs=[VMEM, VMEM],
        scratch_shapes=[
            pltpu.VMEM((4, 512, 1024), BF16),
            pltpu.VMEM((4, 128, 1024), BF16),
            pltpu.VMEM((4, 4, 128, 1024), BF16),
            pltpu.VMEM((4, 1024, 768), BF16),
            pltpu.VMEM((512, 768), F32),
            pltpu.VMEM((4, 512, 256), BF16),
            pltpu.VMEM((16, 4, 2, 128, 128), BF16),
            pltpu.VMEM((512, 256), BF16),
            pltpu.VMEM((4, 1, 512), F32),
            pltpu.VMEM((4, 1, 512), F32),
            pltpu.VMEM((4, 128, 512), F32),
            pltpu.VMEM((4, 128, 512), BF16),
            pltpu.VMEM((4, 128, 512), BF16),
            pltpu.VMEM((4, 144, 512), BF16),
            pltpu.VMEM((4, 16, 512), BF16),
            pltpu.VMEM((4, 16, 512), BF16),
            pltpu.VMEM((512, 1024), BF16),
            pltpu.VMEM((512, 1024), BF16),
            pltpu.VMEM((1024, 512), F32),
            pltpu.VMEM((2, 4, 128, 512), BF16),
            pltpu.VMEM((4, 128, 1024), BF16),
            pltpu.VMEM((4, 128, 1024), BF16),
            pltpu.VMEM((4, 4, 128, 256), BF16),
            pltpu.VMEM((16, 128, 256), BF16),
            pltpu.VMEM((8, 16, 256), BF16),
            pltpu.VMEM((8, 16, 256), BF16),
            pltpu.VMEM((4, 16, 256), F32),
            pltpu.VMEM((16, 1024), BF16),
            pltpu.VMEM((2, 16, 128), F32),
            pltpu.VMEM((8, 16, 128), F32),
            pltpu.VMEM((4, 16, 128), F32),
            DMA((10,)), DMA((3, 4)), DMA((3, 4)), DMA((6,)), DMA((6,)), DMA((6,)), DMA((6,)),
            DMA((8, 4)), DMA((8, 4)), DMA((16, 4)), DMA((4,)), DMA((4,)), DMA, DMA,
            DMA((4,)), DMA((4,)), DMA((16,)), DMA((16,)), DMA((8,)), DMA((8,)), DMA((4,)), DMA((4,)),
            DMA((3,)), DMA, DMA((11,)), DMA((11,)),
        ],
        compiler_params=pltpu.CompilerParams(collective_id=0, has_side_effects=True, vmem_limit_bytes=56 * 1024 * 1024),
        name="window",
    )(ids, gain, wide, wq, wkv, states, grad, wout)


def finish_kernel(rows_ref, gains_ref, out_ref, gout_ref):
    out_ref[...] = rows_ref[...]
    gout_ref[...] = gains_ref[...]


def finish(rows, gains):
    return pl.pallas_call(
        finish_kernel,
        out_shape=[jax.ShapeDtypeStruct((16, 1024), F32), jax.ShapeDtypeStruct((8, 128), F32)],
        in_specs=[VMEM, VMEM],
        out_specs=[VMEM, VMEM],
        name="finish",
    )(rows, gains)


def on_device(byte_states, byte_wide, patch_of, w_query, w_keyval, w_out, norm_gain, out_grad):
    rows, gains = finish(*window(
        patch_of, norm_gain.reshape(8, 128), byte_wide[0], w_query, w_keyval, byte_states[0], out_grad[0], w_out
    ))
    return rows, gains.reshape(1024)


def solution(mesh):
    return jax.shard_map(
        on_device,
        mesh=mesh,
        in_specs=(
            P("fsdp", "seq", None),
            P("fsdp", "seq", None),
            P("fsdp", "seq"),
            P("fsdp", None),
            P("fsdp", None),
            P("fsdp", None),
            P(),
            P("fsdp", "seq", None),
        ),
        out_specs=(P("seq", None), P()),
        check_vma=False,
    )
```

```python
import jax
import jax.numpy as jnp
from jax import lax
from jax.experimental import pallas as pl
from jax.experimental.pallas import tpu as pltpu
from jax.sharding import PartitionSpec as P

E = 128
PCAP = 128
NY, NZ, NX = 4, 8, 4
EPS = 1e-05
DEAD_ROW = 1024.0
DEAD_KEY = 4096.0
NEG = -1e30
Q_SCALE = float(E) ** (-0.5) * 1.4426950408889634
MESH = pl.DeviceIdType.MESH
F32 = jnp.float32
BF16 = jnp.bfloat16


def place():
    seq = lax.axis_index("seq")
    return seq // 16, (seq // 2) % 8, seq % 2, lax.axis_index("fsdp")


def dev(y, z, c, x):
    return {"seq": (y * 8 + z) * 2 + c, "fsdp": x}


def remote(src, dst, send, recv, peer):
    return pltpu.make_async_remote_copy(
        src_ref=src, dst_ref=dst, send_sem=send, recv_sem=recv, device_id=peer, device_id_type=MESH
    )


def dot(a, b, ca=1, cb=0):
    return lax.dot_general(a, b, (((ca,), (cb,)), ((), ())), preferred_element_type=F32)


def iota(shape, axis):
    return lax.broadcasted_iota(jnp.int32, shape, axis)


STEPS = (0, 3, 1, 2)


def window_kernel(ids_ref, gain_ref, wide_ref, wq_ref, wkv_ref, states_hbm, grad_hbm, wout_ref, out_ref, gout_ref,
                  wide_v, pooled, nrm, wbuf, accp, q_ref, blocks, kext, top, total, acc, osend, att, ctx_ref, picks, row_out, row_in,
                  states_ref, grad_ref, sums_t, dec, sib_out, sib_in, xy_out, xy_in, z_out, z_in, xs, wrow, t0, t1, t2,
                  lsem, ysend, yrecv, xsend, xrecv, ssend, srecv, wzsend, wzrecv, zrsend, zrsib, zrrecv, asend, arecv, rsend, rrecv,
                  sbsend, sbrecv, xysend, xyrecv, zsend, zrecv, gsend, grecv, wsend, wrecv, fsend, frecv):
    y, z, c, x = place()
    seq = lax.axis_index("seq")
    me = 2 * z + c
    right, left = dev((y + 1) % 4, z, c, x), dev((y + 3) % 4, z, c, x)
    xright, xleft = dev(y, z, c, (x + 1) % 4), dev(y, z, c, (x + 3) % 4)
    sibling = dev(y, z, 1 - c, x)
    ymates = [dev((y + d) % 4, z, c, x) for d in (1, 2, 3)]
    xmates = [dev(y, z, c, (x + d) % 4) for d in (1, 2, 3)]
    zmates = [dev(y, (z + d) % 8, c, x) for d in range(1, 8)]
    diagonals = [dev((y + dy) % 4, z, c, (x + dx) % 4) for dy in (1, 2, 3) for dx in (1, 2, 3)]
    followers = [{"seq": (16 * i + me + 1) % 64, "fsdp": x} for i in range(4)]
    leaders = [{"seq": (16 * i + me + 63) % 64, "fsdp": x} for i in range(4)]
    dirn = 1 - 2 * c
    za, zb = dev(y, (z + dirn + 8) % 8, c, x), dev(y, (z - dirn + 8) % 8, c, x)
    peers = ymates + xmates + zmates + diagonals + followers + leaders + [sibling]

    loads = [
        pltpu.make_async_copy(wide_ref.at[:, pl.ds(1024 * k, 1024)], wide_v.at[k], lsem.at[3 + k]) for k in range(4)
    ] + [
        pltpu.make_async_copy(wq_ref.at[:, pl.ds(pl.multiple_of(512 * y, 128), 512)], wbuf.at[0, :, pl.ds(0, 512)], lsem.at[0]),
        pltpu.make_async_copy(wkv_ref.at[:, pl.ds(pl.multiple_of(128 * y, 128), 128)], wbuf.at[0, :, pl.ds(512, 128)], lsem.at[1]),
        pltpu.make_async_copy(wkv_ref.at[:, pl.ds(pl.multiple_of(512 + 128 * y, 128), 128)], wbuf.at[0, :, pl.ds(640, 128)], lsem.at[2]),
        pltpu.make_async_copy(states_hbm, states_ref, lsem.at[7]),
        pltpu.make_async_copy(grad_hbm, grad_ref, lsem.at[8]),
    ]
    for load in loads:
        load.start()
    barrier = pltpu.get_barrier_semaphore()
    for peer in peers:
        pl.semaphore_signal(barrier, inc=1, device_id=peer, device_id_type=MESH)

    onehot = (iota((PCAP, 512), 0) == ids_ref[...]).astype(F32)
    sizes = jnp.sum(onehot, axis=1, keepdims=True)
    onehot = onehot.astype(BF16)
    inverse = 1.0 / jnp.maximum(sizes, 1.0)
    squares = jnp.zeros((PCAP, 1), F32)
    for k in range(4):
        loads[k].wait()
        chunk = (dot(onehot, wide_v[k]) * inverse).astype(BF16)
        pooled[k] = chunk
        chunk = chunk.astype(F32)
        squares = squares + jnp.sum(chunk * chunk, axis=1, keepdims=True)
    for load in loads[4:7]:
        load.wait()
    pl.semaphore_wait(barrier, len(peers))

    parity = z % 2

    def part(slot, owner, side, half):
        return wbuf.at[slot, pl.ds(pl.multiple_of(512 * owner + 256 * side + 128 * half, 128), 128)]

    def send_weights(direction, half):
        i = 2 * direction + half
        copy = remote(part(0, c, parity, half), part(1 + direction, c, parity, half),
                      xsend.at[i], xrecv.at[i], (xright, xleft)[direction])
        copy.start()
        return copy

    def send_rows(direction, k):
        copy = remote(nrm.at[k, 0], nrm.at[k, 1 + direction],
                      ysend.at[direction, k], yrecv.at[direction, k], (right, left)[direction])
        copy.start()
        return copy

    warrivals = {}
    for half in range(2):
        for direction in range(2):
            warrivals[direction, half ^ direction] = send_weights(direction, half ^ direction)
    scale = lax.rsqrt(squares / 4096.0 + EPS)
    arrivals = {}
    for k in (0, 3, 1, 2):
        chunk = pooled[k].astype(F32) * scale
        if k == 0:
            chunk = jnp.where((iota((PCAP, 1024), 1) == 0) & (sizes < 0.5), DEAD_ROW, chunk)
        nrm[k, 0] = chunk.astype(BF16)
        direction = 0 if k < 2 else 1
        arrivals[direction, k] = send_rows(direction, k)
    for direction, k in ((0, 2), (1, 1), (0, 3), (1, 0)):
        arrivals[direction, k] = send_rows(direction, k)
    wcopies = [remote(wout_ref.at[pl.ds(pl.multiple_of(16 * me, 16), 16)], wrow, wsend.at[d], wrecv, xmates[d]) for d in range(3)]
    wown = pltpu.make_async_copy(wout_ref.at[pl.ds(pl.multiple_of(16 * me, 16), 16)], wrow, lsem.at[9])

    @pl.when(x == y)
    def _():
        for copy in wcopies:
            copy.start()
        wown.start()

    lasts, wlasts, zgives, ssends = [], [], [], []

    def give(slot, side, half, i):
        copy = remote(part(slot, c, side, half), part(slot, c, side, half), ssend.at[i], srecv.at[i], sibling)
        copy.start()
        ssends.append(copy)

    def spread_weights(slot, half):
        i = 2 * (slot - 1) + half
        copy = remote(part(slot, c, parity, half), part(slot, c, parity, half), wzsend.at[i], wzrecv.at[i],
                      zmates[0] if half == 0 else zmates[6])
        copy.start()
        zgives.append((slot, half, copy))
        give(slot, parity, half, i)

    def pass_rows(direction, k, peer):
        arrivals[direction, k].wait_recv()
        copy = remote(nrm.at[k, 1 + direction], nrm.at[k, 3], ysend.at[2, k], yrecv.at[2, k], peer)
        copy.start()
        lasts.append(copy)

    for direction, half in ((0, 0), (1, 1), (0, 1), (1, 0)):
        warrivals[direction, half].wait_recv()
        if direction == half:
            copy = remote(part(1 + direction, c, parity, half), part(3, c, parity, half),
                          xsend.at[4 + half], xrecv.at[4 + half], (xright, xleft)[direction])
            copy.start()
            wlasts.append(copy)
        spread_weights(1 + direction, half)
    for half, copy in enumerate(wlasts):
        copy.wait_recv()
        spread_weights(3, half)
    for slot, half, copy in zgives:
        copy.wait_recv()
        give(slot, 1 - parity, half, 6 + 2 * (slot - 1) + half)
    pass_rows(0, 0, right)
    pass_rows(1, 3, left)
    pass_rows(0, 1, right)
    pass_rows(1, 2, left)
    for direction, k in ((0, 2), (1, 1), (0, 3), (1, 0)):
        arrivals[direction, k].wait_recv()
    for copy in ssends:
        copy.wait_recv()
    wsends = list(warrivals.values()) + [copy for _, _, copy in zgives]
    ysends = list(arrivals.values())

    ones = (iota((512, 128), 1) == 0).astype(F32).astype(BF16)
    first = []

    def publish(p):
        at = (y + STEPS[p]) % 4
        here = pl.ds(128 * p, 128)
        dead = nrm[0, p][:, 0:128].astype(F32)[:, 0:1] > 512.0
        living = jnp.sum(jnp.where(dead, 0.0, 1.0), axis=0, keepdims=True).astype(jnp.int32)
        picks[at] = (iota((16, PCAP), 1) == living - 1).astype(F32).astype(BF16)
        blocks[0, at, 0] = jnp.where(dead, DEAD_KEY, accp[here, pl.ds(512, 128)]).astype(BF16)
        blocks[0, at, 1] = accp[here, pl.ds(640, 128)].T.astype(BF16)
        for copy in (
            remote(blocks.at[0, at], blocks.at[1, at], zrsend.at[1, p], zrrecv.at[1, p], za),
            remote(blocks.at[0, at], blocks.at[2, at], zrsend.at[2, p], zrrecv.at[2, p], zb),
            remote(blocks.at[0, at], blocks.at[8, at], zrsib.at[0, p], zrrecv.at[8, p], sibling),
        ):
            copy.start()
            first.append(copy)

    def queries(p):
        at = (y + STEPS[p]) % 4
        here = pl.ds(128 * p, 128)
        for g in range(4):
            q_ref[at, pl.ds(128 * g, 128), pl.ds(0, 128)] = (accp[here, pl.ds(128 * g, 128)] * Q_SCALE).astype(BF16)
        q_ref[at, :, pl.ds(128, 128)] = ones

    def arrived(slot, p):
        at = (y + STEPS[p]) % 4
        remote(blocks.at[slot, at], blocks.at[slot, at], zrsend.at[1, p], zrrecv.at[slot, p], sibling).wait_recv()

    def relay(slot, p, peer):
        at = (y + STEPS[p]) % 4
        remote(blocks.at[slot, at], blocks.at[slot + 2, at], zrsend.at[slot + 2, p], zrrecv.at[slot + 2, p], peer).start()

    def share(slot, p):
        at = (y + STEPS[p]) % 4
        remote(blocks.at[slot, at], blocks.at[8 + slot, at], zrsib.at[slot, p], zrrecv.at[8 + slot, p], sibling).start()

    def handle(hop, p):
        arrived(2 * hop - 1, p)

        @pl.when(hop <= 3)
        def _():
            relay(2 * hop - 1, p, za)

        share(2 * hop - 1, p)

        @pl.when(hop <= 3)
        def _():
            arrived(2 * hop, p)

            @pl.when(hop <= 2)
            def _():
                relay(2 * hop, p, zb)

            share(2 * hop, p)

    for at, step in enumerate(STEPS):
        k = (x + step) % 4
        value = dot(nrm[k, 0:3].reshape(384, 1024), wbuf[at])
        if at == 0:
            accp[0:384] = value
        else:
            accp[0:384] += value
    for p in range(3):
        publish(p)
    for p in range(3):
        queries(p)
    for p in range(3):
        handle(1, p)
    for copy in lasts:
        copy.wait_recv()
    for at, step in enumerate(STEPS):
        k = (x + step) % 4
        value = dot(nrm[k, 3], wbuf[at])
        if at == 0:
            accp[384:512] = value
        else:
            accp[384:512] += value
    publish(3)
    queries(3)

    def load_keys(slots):
        for i in range(4):
            for j, slot in enumerate(slots):
                keys = blocks[slot, i, 0]
                here = pl.ds(256 * i + 128 * j, 128)
                kext[here, 0:128] = keys
                dead = keys.astype(F32)[:, 0:1] > 2000.0
                kext[here, 128:256] = jnp.broadcast_to(jnp.where(dead, NEG, 0.0), (128, 128)).astype(BF16)

    def group(slots, work, fresh):
        def score(item):
            yq, count = item
            return dot(kext[0:256 * count], q_ref[yq], 1, 1)

        def soften(item, scores):
            yq, count = item
            if fresh:
                last = scores[256 * (count - 1):]
                reach = jnp.where(iota((256, 512), 0) < 128, iota((256, 512), 1) % 128, 255 * c)
                last = jnp.where(iota((256, 512), 0) <= reach, last, NEG)
                scores = jnp.concatenate([scores[: 256 * (count - 1)], last], axis=0) if count > 1 else last
            peak = jnp.max(scores, axis=0, keepdims=True)
            decay = None
            if not fresh:
                old = top[yq]
                peak = jnp.maximum(peak, old)
                decay = jnp.exp2(old - peak)
            probs = jnp.exp2(scores - peak)
            sums = jnp.sum(probs, axis=0, keepdims=True)
            top[yq] = peak
            total[yq] = sums if fresh else total[yq] * decay + sums
            return probs.astype(BF16), decay

        def mix(item, probs, decay):
            yq, count = item
            values = jnp.concatenate([blocks[slot, i, 1] for i in range(count) for slot in slots], axis=1)
            mixed = dot(values, probs)
            acc[yq] = mixed if fresh else acc[yq] * decay + mixed

        ahead, held = score(work[0]), None
        for i, item in enumerate(work):
            scores = ahead
            if i + 1 < len(work):
                ahead = score(work[i + 1])
            softened = soften(item, scores)
            if held is not None:
                mix(*held)
            held = (item, *softened)
        mix(*held)

    for p in range(4):
        arrived(8, p)
    load_keys((0, 8))
    group((0, 8), [(yq, yq + 1) for yq in range(4)], True)

    def ring(i, carry):
        s = i + 1
        hop = i // 2 + 1
        odd = 1 - i % 2

        @pl.when(odd == 0)
        def _():
            for p in range(4):
                handle(hop + 1, p)

        mate = 7 + s + 2 * odd - s // 7
        for p in range(4):
            arrived(mate, p)
        zsrc = (z - hop * dirn * (2 * odd - 1) + 8) % 8
        load_keys((s, mate))

        @pl.when(zsrc < z)
        def _():
            group((s, mate), [(yq, yq + 1) for yq in range(4)], False)

        @pl.when(zsrc > z)
        def _():
            group((s, mate), [(yq, yq) for yq in range(1, 4)], False)

        return carry

    handle(1, 3)
    lax.fori_loop(0, 7, ring, 0)

    for yq in range(4):
        out = acc[yq] / total[yq]
        for g in range(4):
            osend[yq, :, pl.ds(128 * g, 128)] = out[:, 128 * g:128 * g + 128].T.astype(BF16)
    backs = []
    for d in (2, 1, 3):
        copy = remote(osend.at[(y + d) % 4], att.at[y], asend.at[d], arecv.at[d], ymates[d - 1])
        copy.start()
        backs.append(copy)
    for yq in range(4):
        row_out[yq] = dot(picks[yq], osend[yq]).astype(BF16)
        copy = remote(row_out.at[yq], row_in.at[y], rsend.at[yq], rrecv.at[y], followers[yq])
        copy.start()
        backs.append(copy)
    att[y] = osend[y]
    for d in (1, 3, 2):
        there = (y + 4 - d) % 4
        remote(att.at[there], att.at[there], asend.at[d], arecv.at[d], ymates[d - 1]).wait_recv()

    squares = jnp.zeros((PCAP, 1), F32)
    for h in range(4):
        piece = att[h].astype(F32)
        squares = squares + jnp.sum(piece * piece, axis=1, keepdims=True)
    scale = lax.rsqrt(squares / 2048.0 + EPS)
    ids = ids_ref[...]
    for h in range(4):
        ctx_ref[h, 0:128] = (att[h].astype(F32) * scale).astype(BF16)
    for h in range(4):
        remote(row_in.at[h], row_in.at[h], rsend.at[h], rrecv.at[h], sibling).wait_recv()
    squares = jnp.zeros((16, 1), F32)
    for h in range(4):
        piece = row_in[h].astype(F32)
        squares = squares + jnp.sum(piece * piece, axis=1, keepdims=True)
    scale = lax.rsqrt(squares / 2048.0 + EPS)
    for h in range(4):
        ctx_ref[h, 128:144] = (row_in[h].astype(F32) * scale).astype(BF16)
    for load in loads[7:]:
        load.wait()

    own_hot = iota((144, 512), 0) == ids
    prior_hot = iota((144, 512), 0) == jnp.where(ids > 0, ids - 1, 128)
    has_prior = (ids > 0) | (seq > 0)
    squares = jnp.zeros((1, 512), F32)
    for h in range(8):
        lanes = pl.ds(128 * (h % 4), 128)
        states = states_ref[:, pl.ds(128 * h, 128)].astype(F32).T
        keys = ctx_ref[h // 4, :, lanes]
        values = ctx_ref[2 + h // 4, :, lanes]
        scores = dot(keys, states.astype(BF16)) * Q_SCALE
        own = jnp.sum(jnp.where(own_hot, scores, 0.0), axis=0, keepdims=True)
        prior = jnp.sum(jnp.where(prior_hot, scores, 0.0), axis=0, keepdims=True)
        prior = jnp.where(has_prior, prior, NEG)
        peak = jnp.maximum(own, prior)
        own = jnp.exp2(own - peak)
        prior = jnp.exp2(prior - peak)
        scale = 1.0 / (own + prior)
        weights = jnp.where(own_hot, own * scale, jnp.where(prior_hot, prior * scale, 0.0))
        attn = dot(values, weights.astype(BF16), 0, 0)
        summed = states + attn
        squares = squares + jnp.sum(summed * summed, axis=0, keepdims=True)
        sums_t[pl.ds(128 * h, 128)] = summed
    scale = lax.rsqrt(squares / 1024.0 + EPS)
    for h in range(8):
        gain = jnp.broadcast_to(gain_ref[h:h + 1], (128, 128)).T[:, 0:1]
        decoded = ((sums_t[pl.ds(128 * h, 128)] * scale) * gain).astype(BF16)
        for i in range(8):
            at = (h % 2) * 4 + i // 2
            dec[i % 2, h // 2, pl.ds(16 * at, 16)] = decoded[16 * i:16 * i + 16]

    sib_copies = []
    for i, d in enumerate((2, 1, 3, 0)):
        sib_out[i] = dot(dec[1 - c, (y + d) % 4], grad_ref[...]).astype(BF16)
        copy = remote(sib_out.at[i], sib_in.at[i], sbsend.at[i], sbrecv.at[i], sibling)
        copy.start()
        sib_copies.append(copy)
    xy_copies = []
    for i, d in enumerate((2, 1, 3, 0)):
        mine = dot(dec[c, (y + d) % 4], grad_ref[...])
        sib_copies[i].wait_recv()
        mine = mine + sib_in[i].astype(F32)
        for j in range(4):
            xy_out[d, j] = mine[:, 256 * j:256 * j + 256].astype(BF16)
        for e in (2, 1, 3, 0):
            if d == 0 and e == 0:
                continue
            peer = dev((y + d) % 4, z, c, (x + e) % 4)
            copy = remote(xy_out.at[d, (x + e) % 4], xy_in.at[4 * d + e], xysend.at[4 * d + e], xyrecv.at[4 * d + e], peer)
            copy.start()
            xy_copies.append((4 * d + e, copy))
    mine = xy_out[0, x].astype(F32)
    for i, copy in sorted(xy_copies, key=lambda pair: pair[0]):
        copy.wait_recv()
        mine = mine + xy_in[i].astype(F32)
    z_out[...] = mine.astype(BF16).reshape(8, 16, 256)
    z_copies = []
    for d in (4, 3, 5, 2, 6, 1, 7):
        copy = remote(z_out.at[(z + d) % 8], z_in.at[d], zsend.at[d], zrecv.at[d], zmates[d - 1])
        copy.start()
        z_copies.append((d, copy))
    piece = z_out[z].astype(F32)
    for d, copy in sorted(z_copies, key=lambda pair: pair[0]):
        copy.wait_recv()
        piece = piece + z_in[d].astype(F32)
    xs[x] = piece
    x_copies = []
    for d in (2, 1, 3):
        copy = remote(xs.at[x], xs.at[x], gsend.at[d], grecv.at[d], xmates[d - 1])
        copy.start()
        x_copies.append(copy)

    @pl.when(x == y)
    def _():
        wown.wait()

    @pl.when(x != y)
    def _():
        wcopies[0].wait_recv()

    for d in (1, 3, 2):
        there = (x + 4 - d) % 4
        remote(xs.at[there], xs.at[there], gsend.at[d], grecv.at[d], xmates[d - 1]).wait_recv()

    gains = jnp.zeros((16, 1), F32)
    parts = jnp.zeros((1, 128), F32)
    for j in range(4):
        piece = xs[j]
        gains = gains + jnp.sum(piece * wrow[:, pl.ds(256 * j, 256)].astype(F32), axis=1, keepdims=True)
        power = jnp.sum(piece * piece, axis=0, keepdims=True)
        parts = parts + (power[:, 0:128] + power[:, 128:256])
    lane = (z % 4) * 32 + c * 16
    spread = jnp.where(iota((16, 128), 1) == iota((16, 128), 0) + lane, gains, 0.0)
    spread = jnp.sum(spread, axis=0, keepdims=True)
    row = iota((8, 128), 0)
    t0[0, 0:8] = jnp.where(row == 2 * y + z // 4, spread, 0.0) / gain_ref[...]
    t0[0, 8:16] = jnp.where(row == 0, parts, 0.0)
    f_copies = [remote(t0.at[0], t0.at[1], fsend.at[0], frecv.at[0], sibling)]
    f_copies[0].start()
    f_copies[0].wait_recv()
    t1[z] = t0[0] + t0[1]
    for d in (4, 3, 5, 2, 6, 1, 7):
        copy = remote(t1.at[z], t1.at[z], fsend.at[d], frecv.at[d], zmates[d - 1])
        copy.start()
        f_copies.append(copy)
    for d in range(1, 8):
        there = (z + 8 - d) % 8
        remote(t1.at[there], t1.at[there], fsend.at[d], frecv.at[d], zmates[d - 1]).wait_recv()
    tile = t1[0]
    for i in range(1, 8):
        tile = tile + t1[i]
    t2[y] = tile
    for d in (2, 1, 3):
        copy = remote(t2.at[y], t2.at[y], fsend.at[7 + d], frecv.at[7 + d], ymates[d - 1])
        copy.start()
        f_copies.append(copy)
    for d in (1, 2, 3):
        there = (y + 4 - d) % 4
        remote(t2.at[there], t2.at[there], fsend.at[7 + d], frecv.at[7 + d], ymates[d - 1]).wait_recv()
    tile = (t2[0] + t2[1]) + (t2[2] + t2[3])
    gsum = tile[0:8]
    grand = jnp.sum(tile[8:16] + gsum * gsum, axis=0, keepdims=True)
    grand = jnp.sum(grand, axis=1, keepdims=True)
    clip = jnp.minimum(1.0, 1024.0 / jnp.sqrt(grand))
    for j in range(4):
        out_ref[:, pl.ds(256 * j, 256)] = xs[j] * clip
    gout_ref[...] = gsum * clip

    for copy in (wsends + wlasts + ysends + lasts + ssends + first + backs + sib_copies + x_copies + f_copies
                 + [copy for _, copy in xy_copies] + [copy for _, copy in z_copies]):
        copy.wait_send()

    def drain(s, carry):
        for p in range(4):
            @pl.when(s >= 3)
            def _():
                remote(blocks.at[s, p], blocks.at[s, p], zrsend.at[s, p], zrrecv.at[s, p], sibling).wait_send()
            remote(blocks.at[s, p], blocks.at[s, p], zrsib.at[s, p], zrrecv.at[s, p], sibling).wait_send()
        return carry

    lax.fori_loop(1, 8, drain, 0)

    @pl.when(x == y)
    def _():
        for copy in wcopies:
            copy.wait_send()


VMEM = pl.BlockSpec(memory_space=pltpu.VMEM)
ANY = pl.BlockSpec(memory_space=pl.ANY)
DMA = pltpu.SemaphoreType.DMA


def window(ids, gain, wide, wq, wkv, states, grad, wout):
    return pl.pallas_call(
        window_kernel,
        out_shape=[jax.ShapeDtypeStruct((16, 1024), F32), jax.ShapeDtypeStruct((8, 128), F32)],
        in_specs=[VMEM] * 2 + [ANY] * 6,
        out_specs=[VMEM, VMEM],
        scratch_shapes=[
            pltpu.VMEM((4, 512, 1024), BF16),
            pltpu.VMEM((4, 128, 1024), BF16),
            pltpu.VMEM((4, 4, 128, 1024), BF16),
            pltpu.VMEM((4, 1024, 768), BF16),
            pltpu.VMEM((512, 768), F32),
            pltpu.VMEM((4, 512, 256), BF16),
            pltpu.VMEM((16, 4, 2, 128, 128), BF16),
            pltpu.VMEM((1024, 256), BF16),
            pltpu.VMEM((4, 1, 512), F32),
            pltpu.VMEM((4, 1, 512), F32),
            pltpu.VMEM((4, 128, 512), F32),
            pltpu.VMEM((4, 128, 512), BF16),
            pltpu.VMEM((4, 128, 512), BF16),
            pltpu.VMEM((4, 144, 512), BF16),
            pltpu.VMEM((4, 16, 128), BF16),
            pltpu.VMEM((4, 16, 512), BF16),
            pltpu.VMEM((4, 16, 512), BF16),
            pltpu.VMEM((512, 1024), BF16),
            pltpu.VMEM((512, 1024), BF16),
            pltpu.VMEM((1024, 512), F32),
            pltpu.VMEM((2, 4, 128, 512), BF16),
            pltpu.VMEM((4, 128, 1024), BF16),
            pltpu.VMEM((4, 128, 1024), BF16),
            pltpu.VMEM((4, 4, 128, 256), BF16),
            pltpu.VMEM((16, 128, 256), BF16),
            pltpu.VMEM((8, 16, 256), BF16),
            pltpu.VMEM((8, 16, 256), BF16),
            pltpu.VMEM((4, 16, 256), F32),
            pltpu.VMEM((16, 1024), BF16),
            pltpu.VMEM((2, 16, 128), F32),
            pltpu.VMEM((8, 16, 128), F32),
            pltpu.VMEM((4, 16, 128), F32),
            DMA((10,)), DMA((3, 4)), DMA((3, 4)), DMA((6,)), DMA((6,)), DMA((12,)), DMA((12,)), DMA((6,)), DMA((6,)),
            DMA((8, 4)), DMA((8, 4)), DMA((16, 4)), DMA((4,)), DMA((4,)), DMA((4,)), DMA((4,)),
            DMA((4,)), DMA((4,)), DMA((16,)), DMA((16,)), DMA((8,)), DMA((8,)), DMA((4,)), DMA((4,)),
            DMA((3,)), DMA, DMA((11,)), DMA((11,)),
        ],
        compiler_params=pltpu.CompilerParams(collective_id=0, has_side_effects=True, vmem_limit_bytes=56 * 1024 * 1024),
        name="window",
    )(ids, gain, wide, wq, wkv, states, grad, wout)


def finish_kernel(rows_ref, gains_ref, out_ref, gout_ref):
    out_ref[...] = rows_ref[...]
    gout_ref[...] = gains_ref[...]


def finish(rows, gains):
    return pl.pallas_call(
        finish_kernel,
        out_shape=[jax.ShapeDtypeStruct((16, 1024), F32), jax.ShapeDtypeStruct((8, 128), F32)],
        in_specs=[VMEM, VMEM],
        out_specs=[VMEM, VMEM],
        name="finish",
    )(rows, gains)


def on_device(byte_states, byte_wide, patch_of, w_query, w_keyval, w_out, norm_gain, out_grad):
    rows, gains = finish(*window(
        patch_of, norm_gain.reshape(8, 128), byte_wide[0], w_query, w_keyval, byte_states[0], out_grad[0], w_out
    ))
    return rows, gains.reshape(1024)


def solution(mesh):
    return jax.shard_map(
        on_device,
        mesh=mesh,
        in_specs=(
            P("fsdp", "seq", None),
            P("fsdp", "seq", None),
            P("fsdp", "seq"),
            P("fsdp", None),
            P("fsdp", None),
            P("fsdp", None),
            P(),
            P("fsdp", "seq", None),
        ),
        out_specs=(P("seq", None), P()),
        check_vma=False,
    )
```

```python
import jax
import jax.numpy as jnp
from jax import lax
from jax.experimental import pallas as pl
from jax.experimental.pallas import tpu as pltpu
from jax.sharding import PartitionSpec as P

E = 128
PCAP = 128
NY, NZ, NX = 4, 8, 4
EPS = 1e-05
DEAD_ROW = 1024.0
DEAD_KEY = 4096.0
NEG = -1e30
Q_SCALE = float(E) ** (-0.5) * 1.4426950408889634
MESH = pl.DeviceIdType.MESH
F32 = jnp.float32
BF16 = jnp.bfloat16


def place():
    seq = lax.axis_index("seq")
    return seq // 16, (seq // 2) % 8, seq % 2, lax.axis_index("fsdp")


def dev(y, z, c, x):
    return {"seq": (y * 8 + z) * 2 + c, "fsdp": x}


def remote(src, dst, send, recv, peer):
    return pltpu.make_async_remote_copy(
        src_ref=src, dst_ref=dst, send_sem=send, recv_sem=recv, device_id=peer, device_id_type=MESH
    )


def dot(a, b, ca=1, cb=0):
    return lax.dot_general(a, b, (((ca,), (cb,)), ((), ())), preferred_element_type=F32)


def iota(shape, axis):
    return lax.broadcasted_iota(jnp.int32, shape, axis)


STEPS = (0, 3, 1, 2)


def window_kernel(ids_ref, gain_ref, wide_ref, wq_ref, wkv_ref, states_hbm, grad_hbm, wout_ref, out_ref, gout_ref,
                  wide_v, pooled, nrm, wbuf, accp, q_ref, blocks, kext, top, total, acc, osend, att, ctx_ref, picks, row_out, row_in,
                  states_ref, grad_ref, sums_t, dec, sib_out, sib_in, a_out, b_out, a_in, b_in, a_two, b_two, a_last, b_last, z_out, z_in, xs, wrow, t0, t1, t2,
                  lsem, ysend, yrecv, xsend, xrecv, ssend, srecv, wzsend, wzrecv, zrsend, zrsib, zrrecv, asend, arecv, rsend, rrecv,
                  sbsend, sbrecv, xysend, xyrecv, abxsend, abxrecv, abysend, abyrecv, zsend, zrecv, gsend, grecv, wsend, wrecv, fsend, frecv):
    y, z, c, x = place()
    seq = lax.axis_index("seq")
    me = 2 * z + c
    right, left = dev((y + 1) % 4, z, c, x), dev((y + 3) % 4, z, c, x)
    xright, xleft = dev(y, z, c, (x + 1) % 4), dev(y, z, c, (x + 3) % 4)
    sibling = dev(y, z, 1 - c, x)
    ymates = [dev((y + d) % 4, z, c, x) for d in (1, 2, 3)]
    xmates = [dev(y, z, c, (x + d) % 4) for d in (1, 2, 3)]
    zmates = [dev(y, (z + d) % 8, c, x) for d in range(1, 8)]
    diagonals = [dev((y + dy) % 4, z, c, (x + dx) % 4) for dy in (1, 2, 3) for dx in (1, 2, 3)]
    followers = [{"seq": (16 * i + me + 1) % 64, "fsdp": x} for i in range(4)]
    leaders = [{"seq": (16 * i + me + 63) % 64, "fsdp": x} for i in range(4)]
    dirn = 1 - 2 * c
    za, zb = dev(y, (z + dirn + 8) % 8, c, x), dev(y, (z - dirn + 8) % 8, c, x)
    peers = ymates + xmates + zmates + diagonals + followers + leaders + [sibling]

    loads = [
        pltpu.make_async_copy(wide_ref.at[:, pl.ds(1024 * k, 1024)], wide_v.at[k], lsem.at[3 + k]) for k in range(4)
    ] + [
        pltpu.make_async_copy(wq_ref.at[:, pl.ds(pl.multiple_of(512 * y, 128), 512)], wbuf.at[0, :, pl.ds(0, 512)], lsem.at[0]),
        pltpu.make_async_copy(wkv_ref.at[:, pl.ds(pl.multiple_of(128 * y, 128), 128)], wbuf.at[0, :, pl.ds(512, 128)], lsem.at[1]),
        pltpu.make_async_copy(wkv_ref.at[:, pl.ds(pl.multiple_of(512 + 128 * y, 128), 128)], wbuf.at[0, :, pl.ds(640, 128)], lsem.at[2]),
        pltpu.make_async_copy(states_hbm, states_ref, lsem.at[7]),
        pltpu.make_async_copy(grad_hbm, grad_ref, lsem.at[8]),
    ]
    for load in loads:
        load.start()
    barrier = pltpu.get_barrier_semaphore()
    for peer in peers:
        pl.semaphore_signal(barrier, inc=1, device_id=peer, device_id_type=MESH)

    onehot = (iota((PCAP, 512), 0) == ids_ref[...]).astype(F32)
    sizes = jnp.sum(onehot, axis=1, keepdims=True)
    onehot = onehot.astype(BF16)
    inverse = 1.0 / jnp.maximum(sizes, 1.0)
    squares = jnp.zeros((PCAP, 1), F32)
    for k in range(4):
        loads[k].wait()
        chunk = (dot(onehot, wide_v[k]) * inverse).astype(BF16)
        pooled[k] = chunk
        chunk = chunk.astype(F32)
        squares = squares + jnp.sum(chunk * chunk, axis=1, keepdims=True)
    for load in loads[4:7]:
        load.wait()
    pl.semaphore_wait(barrier, len(peers))

    parity = z % 2

    def part(slot, owner, side, half):
        return wbuf.at[slot, pl.ds(pl.multiple_of(512 * owner + 256 * side + 128 * half, 128), 128)]

    def send_weights(direction, half):
        i = 2 * direction + half
        copy = remote(part(0, c, parity, half), part(1 + direction, c, parity, half),
                      xsend.at[i], xrecv.at[i], (xright, xleft)[direction])
        copy.start()
        return copy

    def send_rows(direction, k):
        copy = remote(nrm.at[k, 0], nrm.at[k, 1 + direction],
                      ysend.at[direction, k], yrecv.at[direction, k], (right, left)[direction])
        copy.start()
        return copy

    warrivals = {}
    for half in range(2):
        for direction in range(2):
            warrivals[direction, half ^ direction] = send_weights(direction, half ^ direction)
    scale = lax.rsqrt(squares / 4096.0 + EPS)
    arrivals = {}
    for k in (0, 3, 1, 2):
        chunk = pooled[k].astype(F32) * scale
        if k == 0:
            chunk = jnp.where((iota((PCAP, 1024), 1) == 0) & (sizes < 0.5), DEAD_ROW, chunk)
        nrm[k, 0] = chunk.astype(BF16)
        direction = 0 if k < 2 else 1
        arrivals[direction, k] = send_rows(direction, k)
    for direction, k in ((0, 2), (1, 1), (0, 3), (1, 0)):
        arrivals[direction, k] = send_rows(direction, k)
    wcopies = [remote(wout_ref.at[pl.ds(pl.multiple_of(16 * me, 16), 16)], wrow, wsend.at[d], wrecv, xmates[d]) for d in range(3)]
    wown = pltpu.make_async_copy(wout_ref.at[pl.ds(pl.multiple_of(16 * me, 16), 16)], wrow, lsem.at[9])

    @pl.when(x == y)
    def _():
        for copy in wcopies:
            copy.start()
        wown.start()

    lasts, wlasts, zgives, ssends = [], [], [], []

    def give(slot, side, half, i):
        copy = remote(part(slot, c, side, half), part(slot, c, side, half), ssend.at[i], srecv.at[i], sibling)
        copy.start()
        ssends.append(copy)

    def spread_weights(slot, half):
        i = 2 * (slot - 1) + half
        copy = remote(part(slot, c, parity, half), part(slot, c, parity, half), wzsend.at[i], wzrecv.at[i],
                      zmates[0] if half == 0 else zmates[6])
        copy.start()
        zgives.append((slot, half, copy))
        give(slot, parity, half, i)

    def pass_rows(direction, k, peer):
        arrivals[direction, k].wait_recv()
        copy = remote(nrm.at[k, 1 + direction], nrm.at[k, 3], ysend.at[2, k], yrecv.at[2, k], peer)
        copy.start()
        lasts.append(copy)

    for direction, half in ((0, 0), (1, 1), (0, 1), (1, 0)):
        warrivals[direction, half].wait_recv()
        if direction == half:
            copy = remote(part(1 + direction, c, parity, half), part(3, c, parity, half),
                          xsend.at[4 + half], xrecv.at[4 + half], (xright, xleft)[direction])
            copy.start()
            wlasts.append(copy)
        spread_weights(1 + direction, half)
    for half, copy in enumerate(wlasts):
        copy.wait_recv()
        spread_weights(3, half)
    for slot, half, copy in zgives:
        copy.wait_recv()
        give(slot, 1 - parity, half, 6 + 2 * (slot - 1) + half)
    pass_rows(0, 0, right)
    pass_rows(1, 3, left)
    pass_rows(0, 1, right)
    pass_rows(1, 2, left)
    for direction, k in ((0, 2), (1, 1), (0, 3), (1, 0)):
        arrivals[direction, k].wait_recv()
    for copy in ssends:
        copy.wait_recv()
    wsends = list(warrivals.values()) + [copy for _, _, copy in zgives]
    ysends = list(arrivals.values())

    ones = (iota((512, 128), 1) == 0).astype(F32).astype(BF16)
    first = []

    def publish(p):
        at = (y + STEPS[p]) % 4
        here = pl.ds(128 * p, 128)
        dead = nrm[0, p][:, 0:128].astype(F32)[:, 0:1] > 512.0
        living = jnp.sum(jnp.where(dead, 0.0, 1.0), axis=0, keepdims=True).astype(jnp.int32)
        picks[at] = (iota((16, PCAP), 1) == living - 1).astype(F32).astype(BF16)
        blocks[0, at, 0] = jnp.where(dead, DEAD_KEY, accp[here, pl.ds(512, 128)]).astype(BF16)
        blocks[0, at, 1] = accp[here, pl.ds(640, 128)].T.astype(BF16)
        for copy in (
            remote(blocks.at[0, at], blocks.at[1, at], zrsend.at[1, p], zrrecv.at[1, p], za),
            remote(blocks.at[0, at], blocks.at[2, at], zrsend.at[2, p], zrrecv.at[2, p], zb),
            remote(blocks.at[0, at], blocks.at[8, at], zrsib.at[0, p], zrrecv.at[8, p], sibling),
        ):
            copy.start()
            first.append(copy)

    def queries(p):
        at = (y + STEPS[p]) % 4
        here = pl.ds(128 * p, 128)
        for g in range(4):
            q_ref[at, pl.ds(128 * g, 128), pl.ds(0, 128)] = (accp[here, pl.ds(128 * g, 128)] * Q_SCALE).astype(BF16)
        q_ref[at, :, pl.ds(128, 128)] = ones

    def arrived(slot, p):
        at = (y + STEPS[p]) % 4
        remote(blocks.at[slot, at], blocks.at[slot, at], zrsend.at[1, p], zrrecv.at[slot, p], sibling).wait_recv()

    def relay(slot, p, peer):
        at = (y + STEPS[p]) % 4
        remote(blocks.at[slot, at], blocks.at[slot + 2, at], zrsend.at[slot + 2, p], zrrecv.at[slot + 2, p], peer).start()

    def share(slot, p):
        at = (y + STEPS[p]) % 4
        remote(blocks.at[slot, at], blocks.at[8 + slot, at], zrsib.at[slot, p], zrrecv.at[8 + slot, p], sibling).start()

    def handle(hop, p):
        arrived(2 * hop - 1, p)

        @pl.when(hop <= 3)
        def _():
            relay(2 * hop - 1, p, za)

        share(2 * hop - 1, p)

        @pl.when(hop <= 3)
        def _():
            arrived(2 * hop, p)

            @pl.when(hop <= 2)
            def _():
                relay(2 * hop, p, zb)

            share(2 * hop, p)

    for at, step in enumerate(STEPS):
        k = (x + step) % 4
        value = dot(nrm[k, 0:3].reshape(384, 1024), wbuf[at])
        if at == 0:
            accp[0:384] = value
        else:
            accp[0:384] += value
    for p in range(3):
        publish(p)
    for p in range(3):
        queries(p)
    for p in range(3):
        handle(1, p)
    for copy in lasts:
        copy.wait_recv()
    for at, step in enumerate(STEPS):
        k = (x + step) % 4
        value = dot(nrm[k, 3], wbuf[at])
        if at == 0:
            accp[384:512] = value
        else:
            accp[384:512] += value
    publish(3)
    queries(3)

    def load_keys(slots):
        for i in range(4):
            for j, slot in enumerate(slots):
                keys = blocks[slot, i, 0]
                here = pl.ds(256 * i + 128 * j, 128)
                kext[here, 0:128] = keys
                dead = keys.astype(F32)[:, 0:1] > 2000.0
                kext[here, 128:256] = jnp.broadcast_to(jnp.where(dead, NEG, 0.0), (128, 128)).astype(BF16)

    def group(slots, work, fresh):
        def score(item):
            yq, count = item
            return dot(kext[0:256 * count], q_ref[yq], 1, 1)

        def soften(item, scores):
            yq, count = item
            if fresh:
                last = scores[256 * (count - 1):]
                reach = jnp.where(iota((256, 512), 0) < 128, iota((256, 512), 1) % 128, 255 * c)
                last = jnp.where(iota((256, 512), 0) <= reach, last, NEG)
                scores = jnp.concatenate([scores[: 256 * (count - 1)], last], axis=0) if count > 1 else last
            peak = jnp.max(scores, axis=0, keepdims=True)
            decay = None
            if not fresh:
                old = top[yq]
                peak = jnp.maximum(peak, old)
                decay = jnp.exp2(old - peak)
            probs = jnp.exp2(scores - peak)
            sums = jnp.sum(probs, axis=0, keepdims=True)
            top[yq] = peak
            total[yq] = sums if fresh else total[yq] * decay + sums
            return probs.astype(BF16), decay

        def mix(item, probs, decay):
            yq, count = item
            values = jnp.concatenate([blocks[slot, i, 1] for i in range(count) for slot in slots], axis=1)
            mixed = dot(values, probs)
            acc[yq] = mixed if fresh else acc[yq] * decay + mixed

        ahead, held = score(work[0]), None
        for i, item in enumerate(work):
            scores = ahead
            if i + 1 < len(work):
                ahead = score(work[i + 1])
            softened = soften(item, scores)
            if held is not None:
                mix(*held)
            held = (item, *softened)
        mix(*held)

    for p in range(4):
        arrived(8, p)
    load_keys((0, 8))
    group((0, 8), [(yq, yq + 1) for yq in range(4)], True)

    def ring(i, carry):
        s = i + 1
        hop = i // 2 + 1
        odd = 1 - i % 2

        @pl.when(odd == 0)
        def _():
            for p in range(4):
                handle(hop + 1, p)

        mate = 7 + s + 2 * odd - s // 7
        for p in range(4):
            arrived(mate, p)
        zsrc = (z - hop * dirn * (2 * odd - 1) + 8) % 8
        load_keys((s, mate))

        @pl.when(zsrc < z)
        def _():
            group((s, mate), [(yq, yq + 1) for yq in range(4)], False)

        @pl.when(zsrc > z)
        def _():
            group((s, mate), [(yq, yq) for yq in range(1, 4)], False)

        return carry

    handle(1, 3)
    lax.fori_loop(0, 7, ring, 0)

    backs = []
    for d in (2, 1, 3, 0):
        yq = (y + d) % 4
        out = acc[yq] / total[yq]
        for g in range(4):
            osend[yq, :, pl.ds(128 * g, 128)] = out[:, 128 * g:128 * g + 128].T.astype(BF16)
        if d > 0:
            copy = remote(osend.at[yq], att.at[y], asend.at[d], arecv.at[d], ymates[d - 1])
            copy.start()
            backs.append(copy)
    for yq in range(4):
        row_out[yq] = dot(picks[yq], osend[yq]).astype(BF16)
        copy = remote(row_out.at[yq], row_in.at[y], rsend.at[yq], rrecv.at[y], followers[yq])
        copy.start()
        backs.append(copy)
    att[y] = osend[y]
    for d in (1, 3, 2):
        there = (y + 4 - d) % 4
        remote(att.at[there], att.at[there], asend.at[d], arecv.at[d], ymates[d - 1]).wait_recv()

    squares = jnp.zeros((PCAP, 1), F32)
    for h in range(4):
        piece = att[h].astype(F32)
        squares = squares + jnp.sum(piece * piece, axis=1, keepdims=True)
    scale = lax.rsqrt(squares / 2048.0 + EPS)
    ids = ids_ref[...]
    for h in range(4):
        ctx_ref[h, 0:128] = (att[h].astype(F32) * scale).astype(BF16)
    for h in range(4):
        remote(row_in.at[h], row_in.at[h], rsend.at[h], rrecv.at[h], sibling).wait_recv()
    squares = jnp.zeros((16, 1), F32)
    for h in range(4):
        piece = row_in[h].astype(F32)
        squares = squares + jnp.sum(piece * piece, axis=1, keepdims=True)
    scale = lax.rsqrt(squares / 2048.0 + EPS)
    for h in range(4):
        ctx_ref[h, 128:144] = (row_in[h].astype(F32) * scale).astype(BF16)
    for load in loads[7:]:
        load.wait()

    own_hot = iota((144, 512), 0) == ids
    prior_hot = iota((144, 512), 0) == jnp.where(ids > 0, ids - 1, 128)
    has_prior = (ids > 0) | (seq > 0)
    squares = jnp.zeros((1, 512), F32)
    for h in range(8):
        lanes = pl.ds(128 * (h % 4), 128)
        states = states_ref[:, pl.ds(128 * h, 128)].astype(F32).T
        keys = ctx_ref[h // 4, :, lanes]
        values = ctx_ref[2 + h // 4, :, lanes]
        scores = dot(keys, states.astype(BF16)) * Q_SCALE
        own = jnp.sum(jnp.where(own_hot, scores, 0.0), axis=0, keepdims=True)
        prior = jnp.sum(jnp.where(prior_hot, scores, 0.0), axis=0, keepdims=True)
        prior = jnp.where(has_prior, prior, NEG)
        peak = jnp.maximum(own, prior)
        own = jnp.exp2(own - peak)
        prior = jnp.exp2(prior - peak)
        scale = 1.0 / (own + prior)
        weights = jnp.where(own_hot, own * scale, jnp.where(prior_hot, prior * scale, 0.0))
        attn = dot(values, weights.astype(BF16), 0, 0)
        summed = states + attn
        squares = squares + jnp.sum(summed * summed, axis=0, keepdims=True)
        sums_t[pl.ds(128 * h, 128)] = summed
    scale = lax.rsqrt(squares / 1024.0 + EPS)
    for h in range(8):
        gain = jnp.broadcast_to(gain_ref[h:h + 1], (128, 128)).T[:, 0:1]
        decoded = ((sums_t[pl.ds(128 * h, 128)] * scale) * gain).astype(BF16)
        for i in range(8):
            at = (h % 2) * 4 + i // 2
            dec[i % 2, h // 2, pl.ds(16 * at, 16)] = decoded[16 * i:16 * i + 16]

    sib_copies = []
    for i, d in enumerate((2, 1, 3, 0)):
        sib_out[i] = dot(dec[1 - c, (y + d) % 4], grad_ref[...]).astype(BF16)
        copy = remote(sib_out.at[i], sib_in.at[i], sbsend.at[i], sbrecv.at[i], sibling)
        copy.start()
        sib_copies.append(copy)
    xy_copies = []
    first_y, first_x = {}, {}
    for i, d in enumerate((2, 1, 3, 0)):
        mine = dot(dec[c, (y + d) % 4], grad_ref[...])
        sib_copies[i].wait_recv()
        mine = mine + sib_in[i].astype(F32)
        for j in range(4):
            a_out[d, j] = mine[:, 256 * j:256 * j + 128].astype(BF16)
            b_out[d, j] = mine[:, 256 * j + 128:256 * j + 256].astype(BF16)
        if d > 0:
            copy = remote(a_out.at[d], a_in.at[d], xysend.at[d], xyrecv.at[d], ymates[d - 1])
            copy.start()
            first_y[d] = copy
        for e in (2, 1, 3):
            copy = remote(b_out.at[d, (x + e) % 4], b_in.at[e, d], xysend.at[4 * e + d], xyrecv.at[4 * e + d], xmates[e - 1])
            copy.start()
            first_x[e, d] = copy
    for d in (1, 3, 2):
        first_y[d].wait_recv()
    for j in range(4):
        a_two[j] = (a_out[0, j].astype(F32) + a_in[1, j].astype(F32) + a_in[2, j].astype(F32) + a_in[3, j].astype(F32)).astype(BF16)
    second_x, second_y = {}, {}
    for e in (2, 1, 3):
        copy = remote(a_two.at[(x + e) % 4], a_last.at[e], abxsend.at[e], abxrecv.at[e], xmates[e - 1])
        copy.start()
        second_x[e] = copy
    for d in (2, 1, 3, 0):
        piece = b_out[d, x].astype(F32)
        for e in (1, 2, 3):
            first_x[e, d].wait_recv()
            piece = piece + b_in[e, d].astype(F32)
        b_two[d] = piece.astype(BF16)
        if d > 0:
            copy = remote(b_two.at[d], b_last.at[d], abysend.at[d], abyrecv.at[d], ymates[d - 1])
            copy.start()
            second_y[d] = copy
    left_half = a_two[x].astype(F32)
    for e in (1, 2, 3):
        second_x[e].wait_recv()
        left_half = left_half + a_last[e].astype(F32)
    right_half = b_two[0].astype(F32)
    for d in (1, 2, 3):
        second_y[d].wait_recv()
        right_half = right_half + b_last[d].astype(F32)
    mine = jnp.concatenate([left_half, right_half], axis=1)
    xy_copies = [(0, copy) for group_of in (first_y, first_x, second_x, second_y) for copy in group_of.values()]
    z_out[...] = mine.astype(BF16).reshape(8, 16, 256)
    z_copies = []
    for d in (4, 3, 5, 2, 6, 1, 7):
        copy = remote(z_out.at[(z + d) % 8], z_in.at[d], zsend.at[d], zrecv.at[d], zmates[d - 1])
        copy.start()
        z_copies.append((d, copy))
    piece = z_out[z].astype(F32)
    for d, copy in sorted(z_copies, key=lambda pair: pair[0]):
        copy.wait_recv()
        piece = piece + z_in[d].astype(F32)
    xs[x] = piece
    x_copies = []
    for d in (2, 1, 3):
        copy = remote(xs.at[x], xs.at[x], gsend.at[d], grecv.at[d], xmates[d - 1])
        copy.start()
        x_copies.append(copy)

    @pl.when(x == y)
    def _():
        wown.wait()

    @pl.when(x != y)
    def _():
        wcopies[0].wait_recv()

    weights = wrow[:, pl.ds(pl.multiple_of(256 * x, 128), 256)].astype(F32)
    gains = jnp.sum(piece * weights, axis=1, keepdims=True)
    power = jnp.sum(piece * piece, axis=0, keepdims=True)
    parts = power[:, 0:128] + power[:, 128:256]
    lane = (z % 4) * 32 + c * 16
    spread = jnp.where(iota((16, 128), 1) == iota((16, 128), 0) + lane, gains, 0.0)
    spread = jnp.sum(spread, axis=0, keepdims=True)
    row = iota((8, 128), 0)
    t0[0, 0:8] = jnp.where(row == 2 * y + z // 4, spread, 0.0) / gain_ref[...]
    t0[0, 8:16] = jnp.where(row == 0, parts, 0.0)
    f_copies = [remote(t0.at[0], t0.at[1], fsend.at[0], frecv.at[0], sibling)]
    f_copies[0].start()
    f_copies[0].wait_recv()
    t1[z] = t0[0] + t0[1]
    for d in (4, 3, 5, 2, 6, 1, 7):
        copy = remote(t1.at[z], t1.at[z], fsend.at[d], frecv.at[d], zmates[d - 1])
        copy.start()
        f_copies.append(copy)
    for d in range(1, 8):
        there = (z + 8 - d) % 8
        remote(t1.at[there], t1.at[there], fsend.at[d], frecv.at[d], zmates[d - 1]).wait_recv()
    tile = t1[0]
    for i in range(1, 8):
        tile = tile + t1[i]
    t2[4 * y + x] = tile
    for i in range(1, 16):
        d, e = i // 4, i % 4
        copy = remote(t2.at[4 * y + x], t2.at[4 * y + x], fsend.at[7 + i], frecv.at[7 + i], dev((y + d) % 4, z, c, (x + e) % 4))
        copy.start()
        f_copies.append(copy)
    for d in (1, 3, 2):
        there = (x + 4 - d) % 4
        remote(xs.at[there], xs.at[there], gsend.at[d], grecv.at[d], xmates[d - 1]).wait_recv()
    for i in range(1, 16):
        there = 4 * ((y + 4 - i // 4) % 4) + (x + 4 - i % 4) % 4
        remote(t2.at[there], t2.at[there], fsend.at[7 + i], frecv.at[7 + i], sibling).wait_recv()
    tile = t2[0]
    for i in range(1, 16):
        tile = tile + t2[i]
    gsum = tile[0:8]
    grand = jnp.sum(tile[8:16] + gsum * gsum, axis=0, keepdims=True)
    grand = jnp.sum(grand, axis=1, keepdims=True)
    clip = jnp.minimum(1.0, 1024.0 / jnp.sqrt(grand))
    for j in range(4):
        out_ref[:, pl.ds(256 * j, 256)] = xs[j] * clip
    gout_ref[...] = gsum * clip

    for copy in (wsends + wlasts + ysends + lasts + ssends + first + backs + sib_copies + x_copies + f_copies
                 + [copy for _, copy in xy_copies] + [copy for _, copy in z_copies]):
        copy.wait_send()

    def drain(s, carry):
        for p in range(4):
            @pl.when(s >= 3)
            def _():
                remote(blocks.at[s, p], blocks.at[s, p], zrsend.at[s, p], zrrecv.at[s, p], sibling).wait_send()
            remote(blocks.at[s, p], blocks.at[s, p], zrsib.at[s, p], zrrecv.at[s, p], sibling).wait_send()
        return carry

    lax.fori_loop(1, 8, drain, 0)

    @pl.when(x == y)
    def _():
        for copy in wcopies:
            copy.wait_send()


VMEM = pl.BlockSpec(memory_space=pltpu.VMEM)
ANY = pl.BlockSpec(memory_space=pl.ANY)
DMA = pltpu.SemaphoreType.DMA


def window(ids, gain, wide, wq, wkv, states, grad, wout):
    return pl.pallas_call(
        window_kernel,
        out_shape=[jax.ShapeDtypeStruct((16, 1024), F32), jax.ShapeDtypeStruct((8, 128), F32)],
        in_specs=[VMEM] * 2 + [ANY] * 6,
        out_specs=[VMEM, VMEM],
        scratch_shapes=[
            pltpu.VMEM((4, 512, 1024), BF16),
            pltpu.VMEM((4, 128, 1024), BF16),
            pltpu.VMEM((4, 4, 128, 1024), BF16),
            pltpu.VMEM((4, 1024, 768), BF16),
            pltpu.VMEM((512, 768), F32),
            pltpu.VMEM((4, 512, 256), BF16),
            pltpu.VMEM((16, 4, 2, 128, 128), BF16),
            pltpu.VMEM((1024, 256), BF16),
            pltpu.VMEM((4, 1, 512), F32),
            pltpu.VMEM((4, 1, 512), F32),
            pltpu.VMEM((4, 128, 512), F32),
            pltpu.VMEM((4, 128, 512), BF16),
            pltpu.VMEM((4, 128, 512), BF16),
            pltpu.VMEM((4, 144, 512), BF16),
            pltpu.VMEM((4, 16, 128), BF16),
            pltpu.VMEM((4, 16, 512), BF16),
            pltpu.VMEM((4, 16, 512), BF16),
            pltpu.VMEM((512, 1024), BF16),
            pltpu.VMEM((512, 1024), BF16),
            pltpu.VMEM((1024, 512), F32),
            pltpu.VMEM((2, 4, 128, 512), BF16),
            pltpu.VMEM((4, 128, 1024), BF16),
            pltpu.VMEM((4, 128, 1024), BF16),
            pltpu.VMEM((4, 4, 128, 128), BF16),
            pltpu.VMEM((4, 4, 128, 128), BF16),
            pltpu.VMEM((4, 4, 128, 128), BF16),
            pltpu.VMEM((4, 4, 128, 128), BF16),
            pltpu.VMEM((4, 128, 128), BF16),
            pltpu.VMEM((4, 128, 128), BF16),
            pltpu.VMEM((4, 128, 128), BF16),
            pltpu.VMEM((4, 128, 128), BF16),
            pltpu.VMEM((8, 16, 256), BF16),
            pltpu.VMEM((8, 16, 256), BF16),
            pltpu.VMEM((4, 16, 256), F32),
            pltpu.VMEM((16, 1024), BF16),
            pltpu.VMEM((2, 16, 128), F32),
            pltpu.VMEM((8, 16, 128), F32),
            pltpu.VMEM((16, 16, 128), F32),
            DMA((10,)), DMA((3, 4)), DMA((3, 4)), DMA((6,)), DMA((6,)), DMA((12,)), DMA((12,)), DMA((6,)), DMA((6,)),
            DMA((8, 4)), DMA((8, 4)), DMA((16, 4)), DMA((4,)), DMA((4,)), DMA((4,)), DMA((4,)),
            DMA((4,)), DMA((4,)), DMA((16,)), DMA((16,)), DMA((4,)), DMA((4,)), DMA((4,)), DMA((4,)), DMA((8,)), DMA((8,)), DMA((4,)), DMA((4,)),
            DMA((3,)), DMA, DMA((23,)), DMA((23,)),
        ],
        compiler_params=pltpu.CompilerParams(collective_id=0, has_side_effects=True, vmem_limit_bytes=56 * 1024 * 1024),
        name="window",
    )(ids, gain, wide, wq, wkv, states, grad, wout)


def finish_kernel(rows_ref, gains_ref, out_ref, gout_ref):
    out_ref[...] = rows_ref[...]
    gout_ref[...] = gains_ref[...]


def finish(rows, gains):
    return pl.pallas_call(
        finish_kernel,
        out_shape=[jax.ShapeDtypeStruct((16, 1024), F32), jax.ShapeDtypeStruct((8, 128), F32)],
        in_specs=[VMEM, VMEM],
        out_specs=[VMEM, VMEM],
        name="finish",
    )(rows, gains)


def on_device(byte_states, byte_wide, patch_of, w_query, w_keyval, w_out, norm_gain, out_grad):
    rows, gains = finish(*window(
        patch_of, norm_gain.reshape(8, 128), byte_wide[0], w_query, w_keyval, byte_states[0], out_grad[0], w_out
    ))
    return rows, gains.reshape(1024)


def solution(mesh):
    return jax.shard_map(
        on_device,
        mesh=mesh,
        in_specs=(
            P("fsdp", "seq", None),
            P("fsdp", "seq", None),
            P("fsdp", "seq"),
            P("fsdp", None),
            P("fsdp", None),
            P("fsdp", None),
            P(),
            P("fsdp", "seq", None),
        ),
        out_specs=(P("seq", None), P()),
        check_vma=False,
    )
```

```python
import jax
import jax.numpy as jnp
from jax import lax
from jax.experimental import pallas as pl
from jax.experimental.pallas import tpu as pltpu
from jax.sharding import PartitionSpec as P

E = 128
PCAP = 128
NY, NZ, NX = 4, 8, 4
EPS = 1e-05
DEAD_ROW = 1024.0
DEAD_KEY = 4096.0
NEG = -1e30
Q_SCALE = float(E) ** (-0.5) * 1.4426950408889634
MESH = pl.DeviceIdType.MESH
F32 = jnp.float32
BF16 = jnp.bfloat16


def place():
    seq = lax.axis_index("seq")
    return seq // 16, (seq // 2) % 8, seq % 2, lax.axis_index("fsdp")


def dev(y, z, c, x):
    return {"seq": (y * 8 + z) * 2 + c, "fsdp": x}


def remote(src, dst, send, recv, peer):
    return pltpu.make_async_remote_copy(
        src_ref=src, dst_ref=dst, send_sem=send, recv_sem=recv, device_id=peer, device_id_type=MESH
    )


def dot(a, b, ca=1, cb=0):
    return lax.dot_general(a, b, (((ca,), (cb,)), ((), ())), preferred_element_type=F32)


def iota(shape, axis):
    return lax.broadcasted_iota(jnp.int32, shape, axis)


STEPS = (0, 3, 1, 2)


def window_kernel(ids_ref, gain_ref, wide_ref, wq_ref, wkv_ref, states_hbm, grad_hbm, wout_ref, out_ref, gout_ref,
                  wide_v, pooled, nrm, wbuf, accp, q_ref, blocks, kext, top, total, acc, osend, att, ctx_ref, picks, row_out, row_in,
                  states_ref, grad_ref, sums_t, dec, sib_out, sib_in, a_out, b_out, a_in, b_in, a_two, b_two, a_last, b_last, z_out, z_in, xs, wrow, t0, t1, t2,
                  lsem, ysend, yrecv, xsend, xrecv, ssend, srecv, wzsend, wzrecv, zrsend, zrsib, zrrecv, asend, arecv, rsend, rrecv,
                  sbsend, sbrecv, xysend, xyrecv, abxsend, abxrecv, abysend, abyrecv, zsend, zrecv, gsend, grecv, wsend, wrecv, fsend, frecv):
    y, z, c, x = place()
    seq = lax.axis_index("seq")
    me = 2 * z + c
    right, left = dev((y + 1) % 4, z, c, x), dev((y + 3) % 4, z, c, x)
    xright, xleft = dev(y, z, c, (x + 1) % 4), dev(y, z, c, (x + 3) % 4)
    sibling = dev(y, z, 1 - c, x)
    ymates = [dev((y + d) % 4, z, c, x) for d in (1, 2, 3)]
    xmates = [dev(y, z, c, (x + d) % 4) for d in (1, 2, 3)]
    zmates = [dev(y, (z + d) % 8, c, x) for d in range(1, 8)]
    diagonals = [dev((y + dy) % 4, z, c, (x + dx) % 4) for dy in (1, 2, 3) for dx in (1, 2, 3)]
    followers = [{"seq": (16 * i + me + 1) % 64, "fsdp": x} for i in range(4)]
    leaders = [{"seq": (16 * i + me + 63) % 64, "fsdp": x} for i in range(4)]
    dirn = 1 - 2 * c
    za, zb = dev(y, (z + dirn + 8) % 8, c, x), dev(y, (z - dirn + 8) % 8, c, x)
    peers = ymates + xmates + zmates + diagonals + followers + leaders + [sibling]

    loads = [
        pltpu.make_async_copy(wide_ref.at[:, pl.ds(1024 * k, 1024)], wide_v.at[k], lsem.at[3 + k]) for k in range(4)
    ] + [
        pltpu.make_async_copy(wq_ref.at[:, pl.ds(pl.multiple_of(512 * y, 128), 512)], wbuf.at[0, :, pl.ds(0, 512)], lsem.at[0]),
        pltpu.make_async_copy(wkv_ref.at[:, pl.ds(pl.multiple_of(128 * y, 128), 128)], wbuf.at[0, :, pl.ds(512, 128)], lsem.at[1]),
        pltpu.make_async_copy(wkv_ref.at[:, pl.ds(pl.multiple_of(512 + 128 * y, 128), 128)], wbuf.at[0, :, pl.ds(640, 128)], lsem.at[2]),
        pltpu.make_async_copy(states_hbm, states_ref, lsem.at[7]),
        pltpu.make_async_copy(grad_hbm, grad_ref, lsem.at[8]),
    ]
    for load in loads:
        load.start()
    barrier = pltpu.get_barrier_semaphore()
    for peer in peers:
        pl.semaphore_signal(barrier, inc=1, device_id=peer, device_id_type=MESH)

    onehot = (iota((PCAP, 512), 0) == ids_ref[...]).astype(F32)
    sizes = jnp.sum(onehot, axis=1, keepdims=True)
    onehot = onehot.astype(BF16)
    inverse = 1.0 / jnp.maximum(sizes, 1.0)
    squares = jnp.zeros((PCAP, 1), F32)
    for k in range(4):
        loads[k].wait()
        chunk = (dot(onehot, wide_v[k]) * inverse).astype(BF16)
        pooled[k] = chunk
        chunk = chunk.astype(F32)
        squares = squares + jnp.sum(chunk * chunk, axis=1, keepdims=True)
    scale = lax.rsqrt(squares / 4096.0 + EPS)
    for k in range(4):
        chunk = pooled[k].astype(F32) * scale
        if k == 0:
            chunk = jnp.where((iota((PCAP, 1024), 1) == 0) & (sizes < 0.5), DEAD_ROW, chunk)
        nrm[k, 0] = chunk.astype(BF16)
    for load in loads[4:7]:
        load.wait()
    pl.semaphore_wait(barrier, len(peers))

    parity = z % 2

    def part(slot, owner, side, half):
        return wbuf.at[slot, pl.ds(pl.multiple_of(512 * owner + 256 * side + 128 * half, 128), 128)]

    def send_weights(direction, half):
        i = 2 * direction + half
        copy = remote(part(0, c, parity, half), part(1 + direction, c, parity, half),
                      xsend.at[i], xrecv.at[i], (xright, xleft)[direction])
        copy.start()
        return copy

    def send_rows(direction, k):
        copy = remote(nrm.at[k, 0], nrm.at[k, 1 + direction],
                      ysend.at[direction, k], yrecv.at[direction, k], (right, left)[direction])
        copy.start()
        return copy

    warrivals = {}
    for half in range(2):
        for direction in range(2):
            warrivals[direction, half ^ direction] = send_weights(direction, half ^ direction)
    arrivals = {}
    for direction, k in ((0, 0), (1, 3), (0, 1), (1, 2), (0, 2), (1, 1), (0, 3), (1, 0)):
        arrivals[direction, k] = send_rows(direction, k)
    wcopies = [remote(wout_ref.at[pl.ds(pl.multiple_of(16 * me, 16), 16)], wrow, wsend.at[d], wrecv, xmates[d]) for d in range(3)]
    wown = pltpu.make_async_copy(wout_ref.at[pl.ds(pl.multiple_of(16 * me, 16), 16)], wrow, lsem.at[9])

    @pl.when(x == y)
    def _():
        for copy in wcopies:
            copy.start()
        wown.start()

    loads[7].wait()
    for h in range(8):
        sums_t[pl.ds(128 * h, 128)] = states_ref[:, pl.ds(128 * h, 128)].astype(F32).T
    lasts, wlasts, zgives, ssends = [], [], [], []

    def give(slot, side, half, i):
        copy = remote(part(slot, c, side, half), part(slot, c, side, half), ssend.at[i], srecv.at[i], sibling)
        copy.start()
        ssends.append(copy)

    def spread_weights(slot, half):
        i = 2 * (slot - 1) + half
        copy = remote(part(slot, c, parity, half), part(slot, c, parity, half), wzsend.at[i], wzrecv.at[i],
                      zmates[0] if half == 0 else zmates[6])
        copy.start()
        zgives.append((slot, half, copy))
        give(slot, parity, half, i)

    def pass_rows(direction, k, peer):
        arrivals[direction, k].wait_recv()
        copy = remote(nrm.at[k, 1 + direction], nrm.at[k, 3], ysend.at[2, k], yrecv.at[2, k], peer)
        copy.start()
        lasts.append(copy)

    for direction, half in ((0, 0), (1, 1), (0, 1), (1, 0)):
        warrivals[direction, half].wait_recv()
        if direction == half:
            copy = remote(part(1 + direction, c, parity, half), part(3, c, parity, half),
                          xsend.at[4 + half], xrecv.at[4 + half], (xright, xleft)[direction])
            copy.start()
            wlasts.append(copy)
        spread_weights(1 + direction, half)
    for half, copy in enumerate(wlasts):
        copy.wait_recv()
        spread_weights(3, half)
    for slot, half, copy in zgives:
        copy.wait_recv()
        give(slot, 1 - parity, half, 6 + 2 * (slot - 1) + half)
    pass_rows(0, 0, right)
    pass_rows(1, 3, left)
    pass_rows(0, 1, right)
    pass_rows(1, 2, left)
    for direction, k in ((0, 2), (1, 1), (0, 3), (1, 0)):
        arrivals[direction, k].wait_recv()
    for copy in ssends:
        copy.wait_recv()
    wsends = list(warrivals.values()) + [copy for _, _, copy in zgives]
    ysends = list(arrivals.values())

    ones = (iota((512, 128), 1) == 0).astype(F32).astype(BF16)
    first = []

    def publish(p):
        at = (y + STEPS[p]) % 4
        here = pl.ds(128 * p, 128)
        dead = nrm[0, p][:, 0:128].astype(F32)[:, 0:1] > 512.0
        living = jnp.sum(jnp.where(dead, 0.0, 1.0), axis=0, keepdims=True).astype(jnp.int32)
        picks[at] = (iota((16, PCAP), 1) == living - 1).astype(F32).astype(BF16)
        blocks[0, at, 0] = jnp.where(dead, DEAD_KEY, accp[here, pl.ds(512, 128)]).astype(BF16)
        blocks[0, at, 1] = accp[here, pl.ds(640, 128)].T.astype(BF16)
        for copy in (
            remote(blocks.at[0, at], blocks.at[1, at], zrsend.at[1, p], zrrecv.at[1, p], za),
            remote(blocks.at[0, at], blocks.at[2, at], zrsend.at[2, p], zrrecv.at[2, p], zb),
            remote(blocks.at[0, at], blocks.at[8, at], zrsib.at[0, p], zrrecv.at[8, p], sibling),
        ):
            copy.start()
            first.append(copy)

    def queries(p):
        at = (y + STEPS[p]) % 4
        here = pl.ds(128 * p, 128)
        for g in range(4):
            q_ref[at, pl.ds(128 * g, 128), pl.ds(0, 128)] = (accp[here, pl.ds(128 * g, 128)] * Q_SCALE).astype(BF16)
        q_ref[at, :, pl.ds(128, 128)] = ones

    def arrived(slot, p):
        at = (y + STEPS[p]) % 4
        remote(blocks.at[slot, at], blocks.at[slot, at], zrsend.at[1, p], zrrecv.at[slot, p], sibling).wait_recv()

    def relay(slot, p, peer):
        at = (y + STEPS[p]) % 4
        remote(blocks.at[slot, at], blocks.at[slot + 2, at], zrsend.at[slot + 2, p], zrrecv.at[slot + 2, p], peer).start()

    def share(slot, p):
        at = (y + STEPS[p]) % 4
        remote(blocks.at[slot, at], blocks.at[8 + slot, at], zrsib.at[slot, p], zrrecv.at[8 + slot, p], sibling).start()

    def handle(hop, p):
        arrived(2 * hop - 1, p)

        @pl.when(hop <= 3)
        def _():
            relay(2 * hop - 1, p, za)

        share(2 * hop - 1, p)

        @pl.when(hop <= 3)
        def _():
            arrived(2 * hop, p)

            @pl.when(hop <= 2)
            def _():
                relay(2 * hop, p, zb)

            share(2 * hop, p)

    def multiply(many, columns):
        left = pl.ds(0, 384) if many else pl.ds(384, 128)
        for at, step in enumerate(STEPS):
            k = (x + step) % 4
            chunk = nrm[k, 0:3].reshape(384, 1024) if many else nrm[k, 3]
            value = dot(chunk, wbuf[at, :, columns])
            if at == 0:
                accp[left, columns] = value
            else:
                accp[left, columns] += value

    multiply(True, pl.ds(512, 256))
    for p in range(3):
        publish(p)
    multiply(True, pl.ds(0, 512))
    for p in range(3):
        queries(p)
    for p in range(3):
        handle(1, p)
    for copy in lasts:
        copy.wait_recv()
    multiply(False, pl.ds(512, 256))
    publish(3)
    multiply(False, pl.ds(0, 512))
    queries(3)

    def load_keys(slots):
        for i in range(4):
            for j, slot in enumerate(slots):
                keys = blocks[slot, i, 0]
                here = pl.ds(256 * i + 128 * j, 128)
                kext[here, 0:128] = keys
                dead = keys.astype(F32)[:, 0:1] > 2000.0
                kext[here, 128:256] = jnp.broadcast_to(jnp.where(dead, NEG, 0.0), (128, 128)).astype(BF16)

    def group(slots, work, fresh):
        def score(item):
            yq, count = item
            return dot(kext[0:256 * count], q_ref[yq], 1, 1)

        def soften(item, scores):
            yq, count = item
            if fresh:
                last = scores[256 * (count - 1):]
                reach = jnp.where(iota((256, 512), 0) < 128, iota((256, 512), 1) % 128, 255 * c)
                last = jnp.where(iota((256, 512), 0) <= reach, last, NEG)
                scores = jnp.concatenate([scores[: 256 * (count - 1)], last], axis=0) if count > 1 else last
            peak = jnp.max(scores, axis=0, keepdims=True)
            decay = None
            if not fresh:
                old = top[yq]
                peak = jnp.maximum(peak, old)
                decay = jnp.exp2(old - peak)
            probs = jnp.exp2(scores - peak)
            sums = jnp.sum(probs, axis=0, keepdims=True)
            top[yq] = peak
            total[yq] = sums if fresh else total[yq] * decay + sums
            return probs.astype(BF16), decay

        def mix(item, probs, decay):
            yq, count = item
            values = jnp.concatenate([blocks[slot, i, 1] for i in range(count) for slot in slots], axis=1)
            mixed = dot(values, probs)
            acc[yq] = mixed if fresh else acc[yq] * decay + mixed

        ahead, held = score(work[0]), None
        for i, item in enumerate(work):
            scores = ahead
            if i + 1 < len(work):
                ahead = score(work[i + 1])
            softened = soften(item, scores)
            if held is not None:
                mix(*held)
            held = (item, *softened)
        mix(*held)

    for p in range(4):
        arrived(8, p)
    load_keys((0, 8))
    group((0, 8), [(yq, yq + 1) for yq in range(4)], True)

    def ring(i, carry):
        s = i + 1
        hop = i // 2 + 1
        odd = 1 - i % 2

        @pl.when(odd == 0)
        def _():
            for p in range(4):
                handle(hop + 1, p)

        mate = 7 + s + 2 * odd - s // 7
        for p in range(4):
            arrived(mate, p)
        zsrc = (z - hop * dirn * (2 * odd - 1) + 8) % 8
        load_keys((s, mate))

        @pl.when(zsrc < z)
        def _():
            group((s, mate), [(yq, yq + 1) for yq in range(4)], False)

        @pl.when(zsrc > z)
        def _():
            group((s, mate), [(yq, yq) for yq in range(1, 4)], False)

        return carry

    handle(1, 3)
    lax.fori_loop(0, 7, ring, 0)

    backs = []
    for d in (2, 1, 3, 0):
        yq = (y + d) % 4
        out = acc[yq] / total[yq]
        for g in range(4):
            osend[yq, :, pl.ds(128 * g, 128)] = out[:, 128 * g:128 * g + 128].T.astype(BF16)
        if d > 0:
            copy = remote(osend.at[yq], att.at[y], asend.at[d], arecv.at[d], ymates[d - 1])
            copy.start()
            backs.append(copy)
    for yq in range(4):
        row_out[yq] = dot(picks[yq], osend[yq]).astype(BF16)
        copy = remote(row_out.at[yq], row_in.at[y], rsend.at[yq], rrecv.at[y], followers[yq])
        copy.start()
        backs.append(copy)
    att[y] = osend[y]
    for d in (1, 3, 2):
        there = (y + 4 - d) % 4
        remote(att.at[there], att.at[there], asend.at[d], arecv.at[d], ymates[d - 1]).wait_recv()

    squares = jnp.zeros((PCAP, 1), F32)
    for h in range(4):
        piece = att[h].astype(F32)
        squares = squares + jnp.sum(piece * piece, axis=1, keepdims=True)
    scale = lax.rsqrt(squares / 2048.0 + EPS)
    ids = ids_ref[...]
    for h in range(4):
        ctx_ref[h, 0:128] = (att[h].astype(F32) * scale).astype(BF16)
    for h in range(4):
        remote(row_in.at[h], row_in.at[h], rsend.at[h], rrecv.at[h], sibling).wait_recv()
    squares = jnp.zeros((16, 1), F32)
    for h in range(4):
        piece = row_in[h].astype(F32)
        squares = squares + jnp.sum(piece * piece, axis=1, keepdims=True)
    scale = lax.rsqrt(squares / 2048.0 + EPS)
    for h in range(4):
        ctx_ref[h, 128:144] = (row_in[h].astype(F32) * scale).astype(BF16)
    loads[8].wait()

    own_hot = iota((144, 512), 0) == ids
    prior_hot = iota((144, 512), 0) == jnp.where(ids > 0, ids - 1, 128)
    has_prior = (ids > 0) | (seq > 0)
    squares = jnp.zeros((1, 512), F32)
    for h in range(8):
        lanes = pl.ds(128 * (h % 4), 128)
        states = sums_t[pl.ds(128 * h, 128)]
        keys = ctx_ref[h // 4, :, lanes]
        values = ctx_ref[2 + h // 4, :, lanes]
        scores = dot(keys, states.astype(BF16)) * Q_SCALE
        own = jnp.sum(jnp.where(own_hot, scores, 0.0), axis=0, keepdims=True)
        prior = jnp.sum(jnp.where(prior_hot, scores, 0.0), axis=0, keepdims=True)
        prior = jnp.where(has_prior, prior, NEG)
        peak = jnp.maximum(own, prior)
        own = jnp.exp2(own - peak)
        prior = jnp.exp2(prior - peak)
        scale = 1.0 / (own + prior)
        weights = jnp.where(own_hot, own * scale, jnp.where(prior_hot, prior * scale, 0.0))
        attn = dot(values, weights.astype(BF16), 0, 0)
        summed = states + attn
        squares = squares + jnp.sum(summed * summed, axis=0, keepdims=True)
        sums_t[pl.ds(128 * h, 128)] = summed
    scale = lax.rsqrt(squares / 1024.0 + EPS)
    for h in range(8):
        gain = jnp.broadcast_to(gain_ref[h:h + 1], (128, 128)).T[:, 0:1]
        decoded = ((sums_t[pl.ds(128 * h, 128)] * scale) * gain).astype(BF16)
        for i in range(8):
            at = (h % 2) * 4 + i // 2
            dec[i % 2, h // 2, pl.ds(16 * at, 16)] = decoded[16 * i:16 * i + 16]

    sib_copies = []
    for i, d in enumerate((2, 1, 3, 0)):
        sib_out[i] = dot(dec[1 - c, (y + d) % 4], grad_ref[...]).astype(BF16)
        copy = remote(sib_out.at[i], sib_in.at[i], sbsend.at[i], sbrecv.at[i], sibling)
        copy.start()
        sib_copies.append(copy)
    xy_copies = []
    first_y, first_x = {}, {}
    for i, d in enumerate((2, 1, 3, 0)):
        mine = dot(dec[c, (y + d) % 4], grad_ref[...])
        sib_copies[i].wait_recv()
        mine = mine + sib_in[i].astype(F32)
        for j in range(4):
            a_out[d, j] = mine[:, 256 * j:256 * j + 128].astype(BF16)
            b_out[d, j] = mine[:, 256 * j + 128:256 * j + 256].astype(BF16)
        if d > 0:
            copy = remote(a_out.at[d], a_in.at[d], xysend.at[d], xyrecv.at[d], ymates[d - 1])
            copy.start()
            first_y[d] = copy
        for e in (2, 1, 3):
            copy = remote(b_out.at[d, (x + e) % 4], b_in.at[e, d], xysend.at[4 * e + d], xyrecv.at[4 * e + d], xmates[e - 1])
            copy.start()
            first_x[e, d] = copy
    for d in (1, 3, 2):
        first_y[d].wait_recv()
    for j in range(4):
        a_two[j] = (a_out[0, j].astype(F32) + a_in[1, j].astype(F32) + a_in[2, j].astype(F32) + a_in[3, j].astype(F32)).astype(BF16)
    second_x, second_y = {}, {}
    for e in (2, 1, 3):
        copy = remote(a_two.at[(x + e) % 4], a_last.at[e], abxsend.at[e], abxrecv.at[e], xmates[e - 1])
        copy.start()
        second_x[e] = copy
    for d in (2, 1, 3, 0):
        piece = b_out[d, x].astype(F32)
        for e in (1, 2, 3):
            first_x[e, d].wait_recv()
            piece = piece + b_in[e, d].astype(F32)
        b_two[d] = piece.astype(BF16)
        if d > 0:
            copy = remote(b_two.at[d], b_last.at[d], abysend.at[d], abyrecv.at[d], ymates[d - 1])
            copy.start()
            second_y[d] = copy
    left_half = a_two[x].astype(F32)
    for e in (1, 2, 3):
        second_x[e].wait_recv()
        left_half = left_half + a_last[e].astype(F32)
    right_half = b_two[0].astype(F32)
    for d in (1, 2, 3):
        second_y[d].wait_recv()
        right_half = right_half + b_last[d].astype(F32)
    mine = jnp.concatenate([left_half, right_half], axis=1)
    xy_copies = [(0, copy) for group_of in (first_y, first_x, second_x, second_y) for copy in group_of.values()]
    z_out[...] = mine.astype(BF16).reshape(8, 16, 256)
    z_copies = []
    for d in (4, 3, 5, 2, 6, 1, 7):
        copy = remote(z_out.at[(z + d) % 8], z_in.at[d], zsend.at[d], zrecv.at[d], zmates[d - 1])
        copy.start()
        z_copies.append((d, copy))
    piece = z_out[z].astype(F32)
    for d, copy in sorted(z_copies, key=lambda pair: pair[0]):
        copy.wait_recv()
        piece = piece + z_in[d].astype(F32)
    xs[x] = piece
    x_copies = []
    for d in (2, 1, 3):
        copy = remote(xs.at[x], xs.at[x], gsend.at[d], grecv.at[d], xmates[d - 1])
        copy.start()
        x_copies.append(copy)

    @pl.when(x == y)
    def _():
        wown.wait()

    @pl.when(x != y)
    def _():
        wcopies[0].wait_recv()

    weights = wrow[:, pl.ds(pl.multiple_of(256 * x, 128), 256)].astype(F32)
    gains = jnp.sum(piece * weights, axis=1, keepdims=True)
    power = jnp.sum(piece * piece, axis=0, keepdims=True)
    parts = power[:, 0:128] + power[:, 128:256]
    lane = (z % 4) * 32 + c * 16
    spread = jnp.where(iota((16, 128), 1) == iota((16, 128), 0) + lane, gains, 0.0)
    spread = jnp.sum(spread, axis=0, keepdims=True)
    row = iota((8, 128), 0)
    t0[0, 0:8] = jnp.where(row == 2 * y + z // 4, spread, 0.0) / gain_ref[...]
    t0[0, 8:16] = jnp.where(row == 0, parts, 0.0)
    f_copies = [remote(t0.at[0], t0.at[1], fsend.at[0], frecv.at[0], sibling)]
    f_copies[0].start()
    f_copies[0].wait_recv()
    t1[z] = t0[0] + t0[1]
    for d in (4, 3, 5, 2, 6, 1, 7):
        copy = remote(t1.at[z], t1.at[z], fsend.at[d], frecv.at[d], zmates[d - 1])
        copy.start()
        f_copies.append(copy)
    for d in range(1, 8):
        there = (z + 8 - d) % 8
        remote(t1.at[there], t1.at[there], fsend.at[d], frecv.at[d], zmates[d - 1]).wait_recv()
    tile = t1[0]
    for i in range(1, 8):
        tile = tile + t1[i]
    t2[4 * y + x] = tile
    for i in range(1, 16):
        d, e = i // 4, i % 4
        copy = remote(t2.at[4 * y + x], t2.at[4 * y + x], fsend.at[7 + i], frecv.at[7 + i], dev((y + d) % 4, z, c, (x + e) % 4))
        copy.start()
        f_copies.append(copy)
    for d in (1, 3, 2):
        there = (x + 4 - d) % 4
        remote(xs.at[there], xs.at[there], gsend.at[d], grecv.at[d], xmates[d - 1]).wait_recv()
    for i in range(1, 16):
        there = 4 * ((y + 4 - i // 4) % 4) + (x + 4 - i % 4) % 4
        remote(t2.at[there], t2.at[there], fsend.at[7 + i], frecv.at[7 + i], sibling).wait_recv()
    tile = t2[0]
    for i in range(1, 16):
        tile = tile + t2[i]
    gsum = tile[0:8]
    grand = jnp.sum(tile[8:16] + gsum * gsum, axis=0, keepdims=True)
    grand = jnp.sum(grand, axis=1, keepdims=True)
    clip = jnp.minimum(1.0, 1024.0 / jnp.sqrt(grand))
    for j in range(4):
        out_ref[:, pl.ds(256 * j, 256)] = xs[j] * clip
    gout_ref[...] = gsum * clip

    for copy in (wsends + wlasts + ysends + lasts + ssends + first + backs + sib_copies + x_copies + f_copies
                 + [copy for _, copy in xy_copies] + [copy for _, copy in z_copies]):
        copy.wait_send()

    def drain(s, carry):
        for p in range(4):
            @pl.when(s >= 3)
            def _():
                remote(blocks.at[s, p], blocks.at[s, p], zrsend.at[s, p], zrrecv.at[s, p], sibling).wait_send()
            remote(blocks.at[s, p], blocks.at[s, p], zrsib.at[s, p], zrrecv.at[s, p], sibling).wait_send()
        return carry

    lax.fori_loop(1, 8, drain, 0)

    @pl.when(x == y)
    def _():
        for copy in wcopies:
            copy.wait_send()


VMEM = pl.BlockSpec(memory_space=pltpu.VMEM)
ANY = pl.BlockSpec(memory_space=pl.ANY)
DMA = pltpu.SemaphoreType.DMA


def window(ids, gain, wide, wq, wkv, states, grad, wout):
    return pl.pallas_call(
        window_kernel,
        out_shape=[jax.ShapeDtypeStruct((16, 1024), F32), jax.ShapeDtypeStruct((8, 128), F32)],
        in_specs=[VMEM] * 2 + [ANY] * 6,
        out_specs=[VMEM, VMEM],
        scratch_shapes=[
            pltpu.VMEM((4, 512, 1024), BF16),
            pltpu.VMEM((4, 128, 1024), BF16),
            pltpu.VMEM((4, 4, 128, 1024), BF16),
            pltpu.VMEM((4, 1024, 768), BF16),
            pltpu.VMEM((512, 768), F32),
            pltpu.VMEM((4, 512, 256), BF16),
            pltpu.VMEM((16, 4, 2, 128, 128), BF16),
            pltpu.VMEM((1024, 256), BF16),
            pltpu.VMEM((4, 1, 512), F32),
            pltpu.VMEM((4, 1, 512), F32),
            pltpu.VMEM((4, 128, 512), F32),
            pltpu.VMEM((4, 128, 512), BF16),
            pltpu.VMEM((4, 128, 512), BF16),
            pltpu.VMEM((4, 144, 512), BF16),
            pltpu.VMEM((4, 16, 128), BF16),
            pltpu.VMEM((4, 16, 512), BF16),
            pltpu.VMEM((4, 16, 512), BF16),
            pltpu.VMEM((512, 1024), BF16),
            pltpu.VMEM((512, 1024), BF16),
            pltpu.VMEM((1024, 512), F32),
            pltpu.VMEM((2, 4, 128, 512), BF16),
            pltpu.VMEM((4, 128, 1024), BF16),
            pltpu.VMEM((4, 128, 1024), BF16),
            pltpu.VMEM((4, 4, 128, 128), BF16),
            pltpu.VMEM((4, 4, 128, 128), BF16),
            pltpu.VMEM((4, 4, 128, 128), BF16),
            pltpu.VMEM((4, 4, 128, 128), BF16),
            pltpu.VMEM((4, 128, 128), BF16),
            pltpu.VMEM((4, 128, 128), BF16),
            pltpu.VMEM((4, 128, 128), BF16),
            pltpu.VMEM((4, 128, 128), BF16),
            pltpu.VMEM((8, 16, 256), BF16),
            pltpu.VMEM((8, 16, 256), BF16),
            pltpu.VMEM((4, 16, 256), F32),
            pltpu.VMEM((16, 1024), BF16),
            pltpu.VMEM((2, 16, 128), F32),
            pltpu.VMEM((8, 16, 128), F32),
            pltpu.VMEM((16, 16, 128), F32),
            DMA((10,)), DMA((3, 4)), DMA((3, 4)), DMA((6,)), DMA((6,)), DMA((12,)), DMA((12,)), DMA((6,)), DMA((6,)),
            DMA((8, 4)), DMA((8, 4)), DMA((16, 4)), DMA((4,)), DMA((4,)), DMA((4,)), DMA((4,)),
            DMA((4,)), DMA((4,)), DMA((16,)), DMA((16,)), DMA((4,)), DMA((4,)), DMA((4,)), DMA((4,)), DMA((8,)), DMA((8,)), DMA((4,)), DMA((4,)),
            DMA((3,)), DMA, DMA((23,)), DMA((23,)),
        ],
        compiler_params=pltpu.CompilerParams(collective_id=0, has_side_effects=True, vmem_limit_bytes=56 * 1024 * 1024),
        name="window",
    )(ids, gain, wide, wq, wkv, states, grad, wout)


def finish_kernel(rows_ref, gains_ref, out_ref, gout_ref):
    out_ref[...] = rows_ref[...]
    gout_ref[...] = gains_ref[...]


def finish(rows, gains):
    return pl.pallas_call(
        finish_kernel,
        out_shape=[jax.ShapeDtypeStruct((16, 1024), F32), jax.ShapeDtypeStruct((8, 128), F32)],
        in_specs=[VMEM, VMEM],
        out_specs=[VMEM, VMEM],
        name="finish",
    )(rows, gains)


def on_device(byte_states, byte_wide, patch_of, w_query, w_keyval, w_out, norm_gain, out_grad):
    rows, gains = finish(*window(
        patch_of, norm_gain.reshape(8, 128), byte_wide[0], w_query, w_keyval, byte_states[0], out_grad[0], w_out
    ))
    return rows, gains.reshape(1024)


def solution(mesh):
    return jax.shard_map(
        on_device,
        mesh=mesh,
        in_specs=(
            P("fsdp", "seq", None),
            P("fsdp", "seq", None),
            P("fsdp", "seq"),
            P("fsdp", None),
            P("fsdp", None),
            P("fsdp", None),
            P(),
            P("fsdp", "seq", None),
        ),
        out_specs=(P("seq", None), P()),
        check_vma=False,
    )
```

```python
import jax
import jax.numpy as jnp
from jax import lax
from jax.experimental import pallas as pl
from jax.experimental.pallas import tpu as pltpu
from jax.sharding import PartitionSpec as P

E = 128
PCAP = 128
NY, NZ, NX = 4, 8, 4
EPS = 1e-05
DEAD_ROW = 1024.0
DEAD_KEY = 4096.0
NEG = -1e30
Q_SCALE = float(E) ** (-0.5) * 1.4426950408889634
MESH = pl.DeviceIdType.MESH
F32 = jnp.float32
BF16 = jnp.bfloat16


def place():
    seq = lax.axis_index("seq")
    return seq // 16, (seq // 2) % 8, seq % 2, lax.axis_index("fsdp")


def dev(y, z, c, x):
    return {"seq": (y * 8 + z) * 2 + c, "fsdp": x}


def remote(src, dst, send, recv, peer):
    return pltpu.make_async_remote_copy(
        src_ref=src, dst_ref=dst, send_sem=send, recv_sem=recv, device_id=peer, device_id_type=MESH
    )


def dot(a, b, ca=1, cb=0):
    return lax.dot_general(a, b, (((ca,), (cb,)), ((), ())), preferred_element_type=F32)


def iota(shape, axis):
    return lax.broadcasted_iota(jnp.int32, shape, axis)


STEPS = (0, 3, 1, 2)


def window_kernel(ids_ref, gain_ref, wide_ref, wq_ref, wkv_ref, states_hbm, grad_hbm, wout_ref, out_ref, gout_ref,
                  wide_v, pooled, nrm, wbuf, accp, q_ref, blocks, kext, top, total, acc, osend, att, ctx_ref, picks, row_out, row_in,
                  states_ref, grad_ref, sums_t, dec, sib_out, sib_in, a_out, b_out, a_in, b_in, a_two, b_two, a_last, b_last, z_out, z_in, xs, wrow, t0, t1, t2,
                  lsem, ysend, yrecv, xsend, xrecv, ssend, srecv, wzsend, wzrecv, zrsend, zrsib, zrrecv, asend, arecv, rsend, rrecv,
                  sbsend, sbrecv, xysend, xyrecv, abxsend, abxrecv, abysend, abyrecv, zsend, zrecv, gsend, grecv, wsend, wrecv, fsend, frecv):
    y, z, c, x = place()
    seq = lax.axis_index("seq")
    me = 2 * z + c
    right, left = dev((y + 1) % 4, z, c, x), dev((y + 3) % 4, z, c, x)
    xright, xleft = dev(y, z, c, (x + 1) % 4), dev(y, z, c, (x + 3) % 4)
    sibling = dev(y, z, 1 - c, x)
    ymates = [dev((y + d) % 4, z, c, x) for d in (1, 2, 3)]
    xmates = [dev(y, z, c, (x + d) % 4) for d in (1, 2, 3)]
    zmates = [dev(y, (z + d) % 8, c, x) for d in range(1, 8)]
    diagonals = [dev((y + dy) % 4, z, c, (x + dx) % 4) for dy in (1, 2, 3) for dx in (1, 2, 3)]
    followers = [{"seq": (16 * i + me + 1) % 64, "fsdp": x} for i in range(4)]
    leaders = [{"seq": (16 * i + me + 63) % 64, "fsdp": x} for i in range(4)]
    dirn = 1 - 2 * c
    za, zb = dev(y, (z + dirn + 8) % 8, c, x), dev(y, (z - dirn + 8) % 8, c, x)
    peers = ymates + xmates + zmates + diagonals + followers + leaders + [sibling]

    loads = [
        pltpu.make_async_copy(wide_ref.at[:, pl.ds(1024 * k, 1024)], wide_v.at[k], lsem.at[3 + k]) for k in range(4)
    ] + [
        pltpu.make_async_copy(wq_ref.at[:, pl.ds(pl.multiple_of(512 * y, 128), 512)], wbuf.at[0, :, pl.ds(0, 512)], lsem.at[0]),
        pltpu.make_async_copy(wkv_ref.at[:, pl.ds(pl.multiple_of(128 * y, 128), 128)], wbuf.at[0, :, pl.ds(512, 128)], lsem.at[1]),
        pltpu.make_async_copy(wkv_ref.at[:, pl.ds(pl.multiple_of(512 + 128 * y, 128), 128)], wbuf.at[0, :, pl.ds(640, 128)], lsem.at[2]),
        pltpu.make_async_copy(states_hbm, states_ref, lsem.at[7]),
        pltpu.make_async_copy(grad_hbm, grad_ref, lsem.at[8]),
    ]
    for load in loads:
        load.start()
    barrier = pltpu.get_barrier_semaphore()
    for peer in peers:
        pl.semaphore_signal(barrier, inc=1, device_id=peer, device_id_type=MESH)

    onehot = (iota((PCAP, 512), 0) == ids_ref[...]).astype(F32)
    sizes = jnp.sum(onehot, axis=1, keepdims=True)
    onehot = onehot.astype(BF16)
    inverse = 1.0 / jnp.maximum(sizes, 1.0)
    squares = jnp.zeros((PCAP, 1), F32)
    for k in range(4):
        loads[k].wait()
        chunk = (dot(onehot, wide_v[k]) * inverse).astype(BF16)
        pooled[k] = chunk
        chunk = chunk.astype(F32)
        squares = squares + jnp.sum(chunk * chunk, axis=1, keepdims=True)
    scale = lax.rsqrt(squares / 4096.0 + EPS)
    for k in range(4):
        chunk = pooled[k].astype(F32) * scale
        if k == 0:
            chunk = jnp.where((iota((PCAP, 1024), 1) == 0) & (sizes < 0.5), DEAD_ROW, chunk)
        nrm[k, 0] = chunk.astype(BF16)
    for load in loads[4:7]:
        load.wait()
    pl.semaphore_wait(barrier, len(peers))

    parity = z % 2

    def part(slot, owner, side, half):
        return wbuf.at[slot, pl.ds(pl.multiple_of(512 * owner + 256 * side + 128 * half, 128), 128)]

    def send_weights(direction, half):
        i = 2 * direction + half
        copy = remote(part(0, c, parity, half), part(1 + direction, c, parity, half),
                      xsend.at[i], xrecv.at[i], (xright, xleft)[direction])
        copy.start()
        return copy

    def send_rows(direction, k):
        copy = remote(nrm.at[k, 0], nrm.at[k, 1 + direction],
                      ysend.at[direction, k], yrecv.at[direction, k], (right, left)[direction])
        copy.start()
        return copy

    warrivals = {}
    for half in range(2):
        for direction in range(2):
            warrivals[direction, half ^ direction] = send_weights(direction, half ^ direction)
    arrivals = {}
    for direction, k in ((0, 0), (1, 3), (0, 1), (1, 2), (0, 2), (1, 1), (0, 3), (1, 0)):
        arrivals[direction, k] = send_rows(direction, k)
    wcopies = [remote(wout_ref.at[pl.ds(pl.multiple_of(16 * me, 16), 16)], wrow, wsend.at[d], wrecv, xmates[d]) for d in range(3)]
    wown = pltpu.make_async_copy(wout_ref.at[pl.ds(pl.multiple_of(16 * me, 16), 16)], wrow, lsem.at[9])

    @pl.when(x == y)
    def _():
        for copy in wcopies:
            copy.start()
        wown.start()

    loads[7].wait()
    for h in range(8):
        sums_t[pl.ds(128 * h, 128)] = states_ref[:, pl.ds(128 * h, 128)].astype(F32).T
    lasts, wlasts, zgives, ssends = [], [], [], []

    def give(slot, side, half, i):
        copy = remote(part(slot, c, side, half), part(slot, c, side, half), ssend.at[i], srecv.at[i], sibling)
        copy.start()
        ssends.append(copy)

    def spread_weights(slot, half):
        i = 2 * (slot - 1) + half
        copy = remote(part(slot, c, parity, half), part(slot, c, parity, half), wzsend.at[i], wzrecv.at[i],
                      zmates[0] if half == 0 else zmates[6])
        copy.start()
        zgives.append((slot, half, copy))
        give(slot, parity, half, i)

    def pass_rows(direction, k, peer):
        arrivals[direction, k].wait_recv()
        copy = remote(nrm.at[k, 1 + direction], nrm.at[k, 3], ysend.at[2, k], yrecv.at[2, k], peer)
        copy.start()
        lasts.append(copy)

    for direction, half in ((0, 0), (1, 1), (0, 1), (1, 0)):
        warrivals[direction, half].wait_recv()
        if direction == half:
            copy = remote(part(1 + direction, c, parity, half), part(3, c, parity, half),
                          xsend.at[4 + half], xrecv.at[4 + half], (xright, xleft)[direction])
            copy.start()
            wlasts.append(copy)
        spread_weights(1 + direction, half)
    for half, copy in enumerate(wlasts):
        copy.wait_recv()
        spread_weights(3, half)
    for slot, half, copy in zgives:
        copy.wait_recv()
        give(slot, 1 - parity, half, 6 + 2 * (slot - 1) + half)
    pass_rows(0, 0, right)
    pass_rows(1, 3, left)
    pass_rows(0, 1, right)
    pass_rows(1, 2, left)
    for direction, k in ((0, 2), (1, 1), (0, 3), (1, 0)):
        arrivals[direction, k].wait_recv()
    for copy in ssends:
        copy.wait_recv()
    wsends = list(warrivals.values()) + [copy for _, _, copy in zgives]
    ysends = list(arrivals.values())

    ones = (iota((512, 128), 1) == 0).astype(F32).astype(BF16)
    first = []

    def publish(p):
        at = (y + STEPS[p]) % 4
        here = pl.ds(128 * p, 128)
        dead = nrm[0, p][:, 0:128].astype(F32)[:, 0:1] > 512.0
        living = jnp.sum(jnp.where(dead, 0.0, 1.0), axis=0, keepdims=True).astype(jnp.int32)
        picks[at] = (iota((16, PCAP), 1) == living - 1).astype(F32).astype(BF16)
        blocks[0, at, 0] = jnp.where(dead, DEAD_KEY, accp[here, pl.ds(512, 128)]).astype(BF16)
        blocks[0, at, 1] = accp[here, pl.ds(640, 128)].T.astype(BF16)
        for copy in (
            remote(blocks.at[0, at], blocks.at[1, at], zrsend.at[1, p], zrrecv.at[1, p], za),
            remote(blocks.at[0, at], blocks.at[2, at], zrsend.at[2, p], zrrecv.at[2, p], zb),
            remote(blocks.at[0, at], blocks.at[8, at], zrsib.at[0, p], zrrecv.at[8, p], sibling),
        ):
            copy.start()
            first.append(copy)

    def queries(p):
        at = (y + STEPS[p]) % 4
        here = pl.ds(128 * p, 128)
        for g in range(4):
            q_ref[at, pl.ds(128 * g, 128), pl.ds(0, 128)] = (accp[here, pl.ds(128 * g, 128)] * Q_SCALE).astype(BF16)
        q_ref[at, :, pl.ds(128, 128)] = ones

    def arrived(slot, p):
        at = (y + STEPS[p]) % 4
        remote(blocks.at[slot, at], blocks.at[slot, at], zrsend.at[1, p], zrrecv.at[slot, p], sibling).wait_recv()

    def relay(slot, p, peer):
        at = (y + STEPS[p]) % 4
        remote(blocks.at[slot, at], blocks.at[slot + 2, at], zrsend.at[slot + 2, p], zrrecv.at[slot + 2, p], peer).start()

    def share(slot, p):
        at = (y + STEPS[p]) % 4
        remote(blocks.at[slot, at], blocks.at[8 + slot, at], zrsib.at[slot, p], zrrecv.at[8 + slot, p], sibling).start()

    def handle(hop, p):
        arrived(2 * hop - 1, p)

        @pl.when(hop <= 3)
        def _():
            relay(2 * hop - 1, p, za)

        share(2 * hop - 1, p)

        @pl.when(hop <= 3)
        def _():
            arrived(2 * hop, p)

            @pl.when(hop <= 2)
            def _():
                relay(2 * hop, p, zb)

            share(2 * hop, p)

    def multiply(many, columns):
        left = pl.ds(0, 384) if many else pl.ds(384, 128)
        for at, step in enumerate(STEPS):
            k = (x + step) % 4
            chunk = nrm[k, 0:3].reshape(384, 1024) if many else nrm[k, 3]
            value = dot(chunk, wbuf[at, :, columns])
            if at == 0:
                accp[left, columns] = value
            else:
                accp[left, columns] += value

    multiply(True, pl.ds(512, 256))
    for p in range(3):
        publish(p)
    multiply(True, pl.ds(0, 512))
    for p in range(3):
        queries(p)
    for p in range(3):
        handle(1, p)
    for copy in lasts:
        copy.wait_recv()
    multiply(False, pl.ds(512, 256))
    publish(3)
    multiply(False, pl.ds(0, 512))
    queries(3)

    def load_keys(slots):
        for i in range(4):
            for j, slot in enumerate(slots):
                keys = blocks[slot, i, 0]
                here = pl.ds(256 * i + 128 * j, 128)
                kext[here, 0:128] = keys
                dead = keys.astype(F32)[:, 0:1] > 2000.0
                kext[here, 128:256] = jnp.broadcast_to(jnp.where(dead, NEG, 0.0), (128, 128)).astype(BF16)

    def group(slots, work, fresh):
        def score(item):
            yq, count = item
            return dot(kext[0:256 * count], q_ref[yq], 1, 1)

        def soften(item, scores):
            yq, count = item
            if fresh:
                last = scores[256 * (count - 1):]
                reach = jnp.where(iota((256, 512), 0) < 128, iota((256, 512), 1) % 128, 255 * c)
                last = jnp.where(iota((256, 512), 0) <= reach, last, NEG)
                scores = jnp.concatenate([scores[: 256 * (count - 1)], last], axis=0) if count > 1 else last
            peak = jnp.max(scores, axis=0, keepdims=True)
            decay = None
            if not fresh:
                old = top[yq]
                peak = jnp.maximum(peak, old)
                decay = jnp.exp2(old - peak)
            probs = jnp.exp2(scores - peak)
            sums = jnp.sum(probs, axis=0, keepdims=True)
            top[yq] = peak
            total[yq] = sums if fresh else total[yq] * decay + sums
            return probs.astype(BF16), decay

        def mix(item, probs, decay):
            yq, count = item
            values = jnp.concatenate([blocks[slot, i, 1] for i in range(count) for slot in slots], axis=1)
            mixed = dot(values, probs)
            acc[yq] = mixed if fresh else acc[yq] * decay + mixed

        ahead, held = score(work[0]), None
        for i, item in enumerate(work):
            scores = ahead
            if i + 1 < len(work):
                ahead = score(work[i + 1])
            softened = soften(item, scores)
            if held is not None:
                mix(*held)
            held = (item, *softened)
        mix(*held)

    for p in range(4):
        arrived(8, p)
    load_keys((0, 8))
    group((0, 8), [(yq, yq + 1) for yq in range(4)], True)

    def ring(i, carry):
        s = i + 1
        hop = i // 2 + 1
        odd = 1 - i % 2

        @pl.when((odd == 1) & (hop <= 3))
        def _():
            for p in range(3):
                handle(hop + 1, p)

        @pl.when(odd == 0)
        def _():
            handle(hop + 1, 3)

        mate = 7 + s + 2 * odd - s // 7
        for p in range(4):
            arrived(mate, p)
        zsrc = (z - hop * dirn * (2 * odd - 1) + 8) % 8
        load_keys((s, mate))

        @pl.when(zsrc < z)
        def _():
            group((s, mate), [(yq, yq + 1) for yq in range(4)], False)

        @pl.when(zsrc > z)
        def _():
            group((s, mate), [(yq, yq) for yq in range(1, 4)], False)

        return carry

    handle(1, 3)
    lax.fori_loop(0, 7, ring, 0)

    backs = []
    for d in (2, 1, 3, 0):
        yq = (y + d) % 4
        out = acc[yq] / total[yq]
        for g in range(4):
            osend[yq, :, pl.ds(128 * g, 128)] = out[:, 128 * g:128 * g + 128].T.astype(BF16)
        if d > 0:
            copy = remote(osend.at[yq], att.at[y], asend.at[d], arecv.at[d], ymates[d - 1])
            copy.start()
            backs.append(copy)
    for yq in range(4):
        row_out[yq] = dot(picks[yq], osend[yq]).astype(BF16)
        copy = remote(row_out.at[yq], row_in.at[y], rsend.at[yq], rrecv.at[y], followers[yq])
        copy.start()
        backs.append(copy)
    att[y] = osend[y]
    for d in (1, 3, 2):
        there = (y + 4 - d) % 4
        remote(att.at[there], att.at[there], asend.at[d], arecv.at[d], ymates[d - 1]).wait_recv()

    squares = jnp.zeros((PCAP, 1), F32)
    for h in range(4):
        piece = att[h].astype(F32)
        squares = squares + jnp.sum(piece * piece, axis=1, keepdims=True)
    scale = lax.rsqrt(squares / 2048.0 + EPS)
    ids = ids_ref[...]
    for h in range(4):
        ctx_ref[h, 0:128] = (att[h].astype(F32) * scale).astype(BF16)
    for h in range(4):
        remote(row_in.at[h], row_in.at[h], rsend.at[h], rrecv.at[h], sibling).wait_recv()
    squares = jnp.zeros((16, 1), F32)
    for h in range(4):
        piece = row_in[h].astype(F32)
        squares = squares + jnp.sum(piece * piece, axis=1, keepdims=True)
    scale = lax.rsqrt(squares / 2048.0 + EPS)
    for h in range(4):
        ctx_ref[h, 128:144] = (row_in[h].astype(F32) * scale).astype(BF16)
    loads[8].wait()

    own_hot = iota((144, 512), 0) == ids
    prior_hot = iota((144, 512), 0) == jnp.where(ids > 0, ids - 1, 128)
    has_prior = (ids > 0) | (seq > 0)
    squares = jnp.zeros((1, 512), F32)
    for h in range(8):
        lanes = pl.ds(128 * (h % 4), 128)
        states = sums_t[pl.ds(128 * h, 128)]
        keys = ctx_ref[h // 4, :, lanes]
        values = ctx_ref[2 + h // 4, :, lanes]
        scores = dot(keys, states.astype(BF16)) * Q_SCALE
        own = jnp.sum(jnp.where(own_hot, scores, 0.0), axis=0, keepdims=True)
        prior = jnp.sum(jnp.where(prior_hot, scores, 0.0), axis=0, keepdims=True)
        prior = jnp.where(has_prior, prior, NEG)
        peak = jnp.maximum(own, prior)
        own = jnp.exp2(own - peak)
        prior = jnp.exp2(prior - peak)
        scale = 1.0 / (own + prior)
        weights = jnp.where(own_hot, own * scale, jnp.where(prior_hot, prior * scale, 0.0))
        attn = dot(values, weights.astype(BF16), 0, 0)
        summed = states + attn
        squares = squares + jnp.sum(summed * summed, axis=0, keepdims=True)
        sums_t[pl.ds(128 * h, 128)] = summed
    scale = lax.rsqrt(squares / 1024.0 + EPS)
    for h in range(8):
        gain = jnp.broadcast_to(gain_ref[h:h + 1], (128, 128)).T[:, 0:1]
        decoded = ((sums_t[pl.ds(128 * h, 128)] * scale) * gain).astype(BF16)
        for i in range(8):
            at = (h % 2) * 4 + i // 2
            dec[i % 2, h // 2, pl.ds(16 * at, 16)] = decoded[16 * i:16 * i + 16]

    sib_copies = []
    for i, d in enumerate((2, 1, 3, 0)):
        sib_out[i] = dot(dec[1 - c, (y + d) % 4], grad_ref[...]).astype(BF16)
        copy = remote(sib_out.at[i], sib_in.at[i], sbsend.at[i], sbrecv.at[i], sibling)
        copy.start()
        sib_copies.append(copy)
    xy_copies = []
    first_y, first_x = {}, {}
    for i, d in enumerate((2, 1, 3, 0)):
        mine = dot(dec[c, (y + d) % 4], grad_ref[...])
        sib_copies[i].wait_recv()
        mine = mine + sib_in[i].astype(F32)
        for j in range(4):
            a_out[d, j] = mine[:, 256 * j:256 * j + 128].astype(BF16)
            b_out[d, j] = mine[:, 256 * j + 128:256 * j + 256].astype(BF16)
        if d > 0:
            copy = remote(a_out.at[d], a_in.at[d], xysend.at[d], xyrecv.at[d], ymates[d - 1])
            copy.start()
            first_y[d] = copy
        for e in (2, 1, 3):
            copy = remote(b_out.at[d, (x + e) % 4], b_in.at[e, d], xysend.at[4 * e + d], xyrecv.at[4 * e + d], xmates[e - 1])
            copy.start()
            first_x[e, d] = copy
    for d in (1, 3, 2):
        first_y[d].wait_recv()
    for j in range(4):
        a_two[j] = (a_out[0, j].astype(F32) + a_in[1, j].astype(F32) + a_in[2, j].astype(F32) + a_in[3, j].astype(F32)).astype(BF16)
    second_x, second_y = {}, {}
    for e in (2, 1, 3):
        copy = remote(a_two.at[(x + e) % 4], a_last.at[e], abxsend.at[e], abxrecv.at[e], xmates[e - 1])
        copy.start()
        second_x[e] = copy
    for d in (2, 1, 3, 0):
        piece = b_out[d, x].astype(F32)
        for e in (1, 2, 3):
            first_x[e, d].wait_recv()
            piece = piece + b_in[e, d].astype(F32)
        b_two[d] = piece.astype(BF16)
        if d > 0:
            copy = remote(b_two.at[d], b_last.at[d], abysend.at[d], abyrecv.at[d], ymates[d - 1])
            copy.start()
            second_y[d] = copy
    left_half = a_two[x].astype(F32)
    for e in (1, 2, 3):
        second_x[e].wait_recv()
        left_half = left_half + a_last[e].astype(F32)
    right_half = b_two[0].astype(F32)
    for d in (1, 2, 3):
        second_y[d].wait_recv()
        right_half = right_half + b_last[d].astype(F32)
    mine = jnp.concatenate([left_half, right_half], axis=1)
    xy_copies = [(0, copy) for group_of in (first_y, first_x, second_x, second_y) for copy in group_of.values()]
    z_out[...] = mine.astype(BF16).reshape(8, 16, 256)
    z_copies = []
    for d in (4, 3, 5, 2, 6, 1, 7):
        copy = remote(z_out.at[(z + d) % 8], z_in.at[d], zsend.at[d], zrecv.at[d], zmates[d - 1])
        copy.start()
        z_copies.append((d, copy))
    piece = z_out[z].astype(F32)
    for d, copy in sorted(z_copies, key=lambda pair: pair[0]):
        copy.wait_recv()
        piece = piece + z_in[d].astype(F32)
    xs[x] = piece
    x_copies = []
    for d in (2, 1, 3):
        copy = remote(xs.at[x], xs.at[x], gsend.at[d], grecv.at[d], xmates[d - 1])
        copy.start()
        x_copies.append(copy)

    @pl.when(x == y)
    def _():
        wown.wait()

    @pl.when(x != y)
    def _():
        wcopies[0].wait_recv()

    weights = wrow[:, pl.ds(pl.multiple_of(256 * x, 128), 256)].astype(F32)
    gains = jnp.sum(piece * weights, axis=1, keepdims=True)
    power = jnp.sum(piece * piece, axis=0, keepdims=True)
    parts = power[:, 0:128] + power[:, 128:256]
    lane = (z % 4) * 32 + c * 16
    spread = jnp.where(iota((16, 128), 1) == iota((16, 128), 0) + lane, gains, 0.0)
    spread = jnp.sum(spread, axis=0, keepdims=True)
    row = iota((8, 128), 0)
    t0[0, 0:8] = jnp.where(row == 2 * y + z // 4, spread, 0.0) / gain_ref[...]
    t0[0, 8:16] = jnp.where(row == 0, parts, 0.0)
    f_copies = [remote(t0.at[0], t0.at[1], fsend.at[0], frecv.at[0], sibling)]
    f_copies[0].start()
    f_copies[0].wait_recv()
    t1[z] = t0[0] + t0[1]
    for d in (4, 3, 5, 2, 6, 1, 7):
        copy = remote(t1.at[z], t1.at[z], fsend.at[d], frecv.at[d], zmates[d - 1])
        copy.start()
        f_copies.append(copy)
    for d in range(1, 8):
        there = (z + 8 - d) % 8
        remote(t1.at[there], t1.at[there], fsend.at[d], frecv.at[d], zmates[d - 1]).wait_recv()
    tile = t1[0]
    for i in range(1, 8):
        tile = tile + t1[i]
    t2[4 * y + x] = tile
    for i in range(1, 16):
        d, e = i // 4, i % 4
        copy = remote(t2.at[4 * y + x], t2.at[4 * y + x], fsend.at[7 + i], frecv.at[7 + i], dev((y + d) % 4, z, c, (x + e) % 4))
        copy.start()
        f_copies.append(copy)
    for d in (1, 3, 2):
        there = (x + 4 - d) % 4
        remote(xs.at[there], xs.at[there], gsend.at[d], grecv.at[d], xmates[d - 1]).wait_recv()
    for i in range(1, 16):
        there = 4 * ((y + 4 - i // 4) % 4) + (x + 4 - i % 4) % 4
        remote(t2.at[there], t2.at[there], fsend.at[7 + i], frecv.at[7 + i], sibling).wait_recv()
    tile = t2[0]
    for i in range(1, 16):
        tile = tile + t2[i]
    gsum = tile[0:8]
    grand = jnp.sum(tile[8:16] + gsum * gsum, axis=0, keepdims=True)
    grand = jnp.sum(grand, axis=1, keepdims=True)
    clip = jnp.minimum(1.0, 1024.0 / jnp.sqrt(grand))
    for j in range(4):
        out_ref[:, pl.ds(256 * j, 256)] = xs[j] * clip
    gout_ref[...] = gsum * clip

    for copy in (wsends + wlasts + ysends + lasts + ssends + first + backs + sib_copies + x_copies + f_copies
                 + [copy for _, copy in xy_copies] + [copy for _, copy in z_copies]):
        copy.wait_send()

    def drain(s, carry):
        for p in range(4):
            @pl.when(s >= 3)
            def _():
                remote(blocks.at[s, p], blocks.at[s, p], zrsend.at[s, p], zrrecv.at[s, p], sibling).wait_send()
            remote(blocks.at[s, p], blocks.at[s, p], zrsib.at[s, p], zrrecv.at[s, p], sibling).wait_send()
        return carry

    lax.fori_loop(1, 8, drain, 0)

    @pl.when(x == y)
    def _():
        for copy in wcopies:
            copy.wait_send()


VMEM = pl.BlockSpec(memory_space=pltpu.VMEM)
ANY = pl.BlockSpec(memory_space=pl.ANY)
DMA = pltpu.SemaphoreType.DMA


def window(ids, gain, wide, wq, wkv, states, grad, wout):
    return pl.pallas_call(
        window_kernel,
        out_shape=[jax.ShapeDtypeStruct((16, 1024), F32), jax.ShapeDtypeStruct((8, 128), F32)],
        in_specs=[VMEM] * 2 + [ANY] * 6,
        out_specs=[VMEM, VMEM],
        scratch_shapes=[
            pltpu.VMEM((4, 512, 1024), BF16),
            pltpu.VMEM((4, 128, 1024), BF16),
            pltpu.VMEM((4, 4, 128, 1024), BF16),
            pltpu.VMEM((4, 1024, 768), BF16),
            pltpu.VMEM((512, 768), F32),
            pltpu.VMEM((4, 512, 256), BF16),
            pltpu.VMEM((16, 4, 2, 128, 128), BF16),
            pltpu.VMEM((1024, 256), BF16),
            pltpu.VMEM((4, 1, 512), F32),
            pltpu.VMEM((4, 1, 512), F32),
            pltpu.VMEM((4, 128, 512), F32),
            pltpu.VMEM((4, 128, 512), BF16),
            pltpu.VMEM((4, 128, 512), BF16),
            pltpu.VMEM((4, 144, 512), BF16),
            pltpu.VMEM((4, 16, 128), BF16),
            pltpu.VMEM((4, 16, 512), BF16),
            pltpu.VMEM((4, 16, 512), BF16),
            pltpu.VMEM((512, 1024), BF16),
            pltpu.VMEM((512, 1024), BF16),
            pltpu.VMEM((1024, 512), F32),
            pltpu.VMEM((2, 4, 128, 512), BF16),
            pltpu.VMEM((4, 128, 1024), BF16),
            pltpu.VMEM((4, 128, 1024), BF16),
            pltpu.VMEM((4, 4, 128, 128), BF16),
            pltpu.VMEM((4, 4, 128, 128), BF16),
            pltpu.VMEM((4, 4, 128, 128), BF16),
            pltpu.VMEM((4, 4, 128, 128), BF16),
            pltpu.VMEM((4, 128, 128), BF16),
            pltpu.VMEM((4, 128, 128), BF16),
            pltpu.VMEM((4, 128, 128), BF16),
            pltpu.VMEM((4, 128, 128), BF16),
            pltpu.VMEM((8, 16, 256), BF16),
            pltpu.VMEM((8, 16, 256), BF16),
            pltpu.VMEM((4, 16, 256), F32),
            pltpu.VMEM((16, 1024), BF16),
            pltpu.VMEM((2, 16, 128), F32),
            pltpu.VMEM((8, 16, 128), F32),
            pltpu.VMEM((16, 16, 128), F32),
            DMA((10,)), DMA((3, 4)), DMA((3, 4)), DMA((6,)), DMA((6,)), DMA((12,)), DMA((12,)), DMA((6,)), DMA((6,)),
            DMA((8, 4)), DMA((8, 4)), DMA((16, 4)), DMA((4,)), DMA((4,)), DMA((4,)), DMA((4,)),
            DMA((4,)), DMA((4,)), DMA((16,)), DMA((16,)), DMA((4,)), DMA((4,)), DMA((4,)), DMA((4,)), DMA((8,)), DMA((8,)), DMA((4,)), DMA((4,)),
            DMA((3,)), DMA, DMA((23,)), DMA((23,)),
        ],
        compiler_params=pltpu.CompilerParams(collective_id=0, has_side_effects=True, vmem_limit_bytes=56 * 1024 * 1024),
        name="window",
    )(ids, gain, wide, wq, wkv, states, grad, wout)


def finish_kernel(rows_ref, gains_ref, out_ref, gout_ref):
    out_ref[...] = rows_ref[...]
    gout_ref[...] = gains_ref[...]


def finish(rows, gains):
    return pl.pallas_call(
        finish_kernel,
        out_shape=[jax.ShapeDtypeStruct((16, 1024), F32), jax.ShapeDtypeStruct((8, 128), F32)],
        in_specs=[VMEM, VMEM],
        out_specs=[VMEM, VMEM],
        name="finish",
    )(rows, gains)


def on_device(byte_states, byte_wide, patch_of, w_query, w_keyval, w_out, norm_gain, out_grad):
    rows, gains = finish(*window(
        patch_of, norm_gain.reshape(8, 128), byte_wide[0], w_query, w_keyval, byte_states[0], out_grad[0], w_out
    ))
    return rows, gains.reshape(1024)


def solution(mesh):
    return jax.shard_map(
        on_device,
        mesh=mesh,
        in_specs=(
            P("fsdp", "seq", None),
            P("fsdp", "seq", None),
            P("fsdp", "seq"),
            P("fsdp", None),
            P("fsdp", None),
            P("fsdp", None),
            P(),
            P("fsdp", "seq", None),
        ),
        out_specs=(P("seq", None), P()),
        check_vma=False,
    )
```
